32 devices in a mesh: batch: 4 (over y, core), table: 8 (over z, x).
Axes of the slice: x: 2, y: 2, z: 4, core: 2. Of those that a mesh axis runs over, the one named last changes fastest.
Arguments:
- tables: bfloat16 [16, 16384, 128], P('table'), may hold values from -8 to 8
- feature_ids: int32 [16384, 16, 8], P('batch', 'table'), may hold values from 0 to 16383
- bag_lengths: int32 [16384, 16], P('batch', 'table'), may hold values from 1 to 8
- feature_slot: int32 [16], replicated, may hold values from 0 to 15, each once
- w_first: bfloat16 [2048, 1024], P('batch'), may hold values from -0.125 to 0.125
- b_first: float32 [1024], replicated, may hold values from -4 to 4
- w_second: bfloat16 [1024, 256], replicated, may hold values from -0.1875 to 0.1875
- bank: bfloat16 [512, 64, 256], P('table'), may hold values from -6 to 6
- log_q: bfloat16 [512, 64], P('table'), may hold values from -12 to -4
- noise_lists: int32 [4, 32], P('batch'), may hold values from 0 to 511, as said below
- pos_items: int32 [16384], P(('batch', 'table')), may hold values from 0 to 32767
Outputs:
- loss: float32 [16384], P(('batch', 'table'))
- pooled_grad: bfloat16 [16384, 16, 128], P('batch', 'table')
The draws below stay inside these ranges and needn't reach their ends.
Inputs may be any that keep to these rules, and one draw needn't show every extreme that they name: `noise_lists`: block ids t * 64 to (t + 1) * 64 - 1 belong to owner t. Each row names 32 distinct blocks, at most 8 of one owner, and exactly 8 of some owner.
All inputs are finite; a program needn't handle non-finite values.
Results may differ from the reference program's by a relative error of at most 0.012.
The reference program's roundings to bfloat16 on the way count: a program that leaves them out, or rounds other values in their place, can miss the bound.
Values may be sent and summed in bfloat16 or wider, within the bound.
No kernel may reach another device: no remote copies, remote signals or barrier semaphores. Data moves between devices by JAX's collectives and lax.ppermute only.
A program may use at most 192 MiB of HBM per device.

```python
import math
import jax
import jax.numpy as jnp
import numpy as np
from jax import lax

E = 128
HID = 1024
DOUT = 256
ROWS = 16384
BAG = 8
BS = 64
BLK_DEV = 64
MOST = 8
NT = 16
NS = 32
NBLK = 512
NITEMS = 32768
U_ROW = 4096
USERS = 16384
N_BATCH = 4
N_TABLE = 8


def draw_tables(key, part):
    key = jax.random.fold_in(key, 7)
    first = jax.random.fold_in(key, 0)
    values = 0.5 * jax.random.normal(first, (NT, ROWS, E), jnp.float32)
    return jnp.clip(values, -8.0, 8.0).astype(jnp.bfloat16)


def draw_noise_lists(key, part):
    key = jax.random.fold_in(key, 5)

    def one_list(inner):
        first, second, third = jax.random.split(inner, 3)
        owner_order = jax.random.permutation(first, N_TABLE)
        change = jnp.zeros((N_TABLE,), jnp.int32)
        change = change.at[0].set(4).at[1:5].set(-1).at[5].set(2).at[6].set(-2)
        counts = jnp.zeros((N_TABLE,), jnp.int32).at[owner_order].set(4 + change)
        local = jax.vmap(lambda kk: jax.random.permutation(kk, BLK_DEV))(jax.random.split(second, N_TABLE))
        block_ids = jnp.arange(N_TABLE, dtype=jnp.int32)[:, None] * BLK_DEV + local[:, :MOST].astype(jnp.int32)
        usable = jnp.arange(MOST, dtype=jnp.int32)[None, :] < counts[:, None]
        ranked = jnp.argsort(1 - usable.reshape(-1).astype(jnp.int32), stable=True)[:NS]
        chosen = block_ids.reshape(-1)[ranked]
        return chosen[jax.random.permutation(third, NS)].astype(jnp.int32)
    return jax.vmap(one_list)(jax.random.split(key, N_BATCH))


def set_ends(values, key, low, largest):
    longest = values.shape.index(max(values.shape))
    spots = []
    for shift in (0, 1):
        where = [jax.random.randint(jax.random.fold_in(key, axis), (), 0, length) for axis, length in enumerate(values.shape)]
        where[longest] = (where[longest] + shift) % values.shape[longest]
        spots.append(tuple(where))
    return values.at[spots[0]].set(low).at[spots[1]].set(largest)


def levels(own_key, shape, pieces, low, high):
    def one(dim, blocks):
        heights = jax.random.uniform(jax.random.fold_in(jax.random.fold_in(own_key, 6), dim), (blocks,), jnp.float32, low / len(pieces), high / len(pieces))
        return jnp.repeat(jnp.exp(heights), shape[dim] // blocks).reshape((-1,) + (1,) * (len(shape) - dim - 1))

    loudness = one(*pieces[0])
    for cut in pieces[1:]:
        loudness = loudness * one(*cut)
    return loudness


def rank_table(count, lean):
    loads = [(1 << 20) // math.isqrt(grade ** lean) + 1 for grade in range(1, count + 1)]
    scale = 1 + sum(loads) // (1 << 30)
    return np.cumsum(np.array([max(1, weight // scale) for weight in loads]))


def skewed_ids(key, dims, amount, slope):
    grid = rank_table(amount, slope)
    ticket = jax.random.randint(jax.random.fold_in(key, 1), dims, 0, int(grid[amount - 1]))
    rank = jnp.searchsorted(jnp.asarray(grid, jnp.int32), ticket, side="right")
    return jax.random.permutation(jax.random.fold_in(key, 2), amount)[rank].astype(jnp.int32)


def centred(key, dims, scale, reach, cuts=(), held_as=jnp.bfloat16):
    values = jax.random.normal(key, dims, jnp.float32) * scale
    if len(cuts) > 0:
        values = levels(key, dims, cuts, -0.22, 0.18) * values
    return jnp.clip(values, min=-reach, max=reach).astype(held_as)


def setup_inputs(seed: int = 0) -> dict:
    splits = jax.random.split(jax.random.key(seed), 12)
    return {
        "tables": draw_tables(jax.random.fold_in(splits[11], 71), 0),
        "feature_ids": set_ends(skewed_ids(splits[1], (USERS, NT, BAG), ROWS, 2), jax.random.fold_in(splits[1], 3), 0, ROWS - 1).astype(jnp.int32),
        "bag_lengths": set_ends(jax.random.randint(splits[2], (USERS, NT), 1, BAG + 1), jax.random.fold_in(splits[2], 1), 1, BAG).astype(jnp.int32),
        "feature_slot": jax.random.permutation(splits[3], NT).astype(jnp.int32),
        "w_first": centred(splits[4], (NT * E, HID), (NT * E) ** -0.5, 0.125, ((0, 4),)),
        "b_first": centred(splits[5], (HID,), 1.0, 4.0, (), jnp.float32),
        "w_second": centred(splits[6], (HID, DOUT), HID ** -0.5, 0.1875),
        "bank": centred(splits[7], (NBLK, BS, DOUT), 1.0, 6.0, ((0, 8),)),
        "log_q": jnp.clip(-12.0 + 8.0 * jax.random.uniform(splits[8], (NBLK, BS), jnp.float32) ** levels(splits[8], (NBLK, BS), ((0, 8),), -0.2, 0.2), -12.0, -4.0).astype(jnp.bfloat16),
        "noise_lists": draw_noise_lists(jax.random.fold_in(splits[11], 71), 0),
        "pos_items": set_ends(skewed_ids(splits[10], (USERS,), NITEMS, 2), jax.random.fold_in(splits[10], 3), 0, NITEMS - 1).astype(jnp.int32),
    }


def reference(tables, feature_ids, bag_lengths, feature_slot, w_first, b_first, w_second, bank, log_q, noise_lists, pos_items):
    scale = DOUT ** -0.5
    flat_bank = bank.reshape(NBLK * BS, DOUT)
    flat_lq = log_q.reshape(NBLK * BS).astype(jnp.float32)
    order = jnp.argsort(feature_slot)
    width = math.gcd(512, U_ROW)
    lanes = jnp.arange(NT)[None, :]

    def one_row(shard):
        start = (shard * U_ROW).astype(jnp.int32)
        row_items = lax.dynamic_slice_in_dim(pos_items, start, U_ROW)
        pos_vec = flat_bank[row_items]
        pos_lq = flat_lq[row_items]
        picked_blocks = noise_lists[shard]
        noise_vec = bank[picked_blocks].reshape(NS * BS, DOUT)
        noise_lq = log_q[picked_blocks].reshape(NS * BS).astype(jnp.float32)
        ids_row = lax.dynamic_slice_in_dim(feature_ids, start, U_ROW).reshape(U_ROW // width, width, NT, BAG)
        lens_row = lax.dynamic_slice_in_dim(bag_lengths, start, U_ROW).reshape(U_ROW // width, width, NT)
        own_row = jnp.arange(U_ROW, dtype=jnp.int32).reshape(U_ROW // width, width)

        def one_block(parts):
            ids, lens, own = parts
            total = jnp.zeros((width, NT, E), jnp.float32)
            for step in range(BAG):
                rows = tables[lanes, ids[:, :, step]].astype(jnp.float32)
                total = total + jnp.where((lens > step)[:, :, None], rows, 0.0)
            pooled = total.astype(jnp.bfloat16)
            features = pooled[:, order, :].reshape(width, NT * E)
            pre = jnp.dot(features, w_first, preferred_element_type=jnp.float32) + b_first
            hidden = jax.nn.silu(pre).astype(jnp.bfloat16)
            user_vec = jnp.dot(hidden, w_second, preferred_element_type=jnp.float32).astype(jnp.bfloat16)
            score_pos = jnp.dot(user_vec, pos_vec.T, preferred_element_type=jnp.float32) * scale - pos_lq
            score_noise = jnp.dot(user_vec, noise_vec.T, preferred_element_type=jnp.float32) * scale - noise_lq
            top = jnp.maximum(jnp.max(score_pos, axis=1), jnp.max(score_noise, axis=1))
            exp_pos = jnp.exp(score_pos - top[:, None])
            exp_noise = jnp.exp(score_noise - top[:, None])
            denom = jnp.sum(exp_pos, axis=1) + jnp.sum(exp_noise, axis=1)
            own_logit = jnp.take_along_axis(score_pos, own[:, None], axis=1)[:, 0]
            loss = top + jnp.log(denom) - own_logit
            prob_pos = (exp_pos / denom[:, None]).astype(jnp.bfloat16)
            prob_noise = (exp_noise / denom[:, None]).astype(jnp.bfloat16)
            mixed = jnp.dot(prob_pos, pos_vec, preferred_element_type=jnp.float32)
            mixed = mixed + jnp.dot(prob_noise, noise_vec, preferred_element_type=jnp.float32)
            user_grad = ((mixed - pos_vec[own].astype(jnp.float32)) * scale).astype(jnp.bfloat16)
            hidden_grad = jnp.dot(user_grad, w_second.T, preferred_element_type=jnp.float32)
            sig = jax.nn.sigmoid(pre)
            pre_grad = (hidden_grad * sig * (1.0 + pre * (1.0 - sig))).astype(jnp.bfloat16)
            feature_grad = jnp.dot(pre_grad, w_first.T, preferred_element_type=jnp.float32).astype(jnp.bfloat16)
            return loss, feature_grad.reshape(width, NT, E)[:, feature_slot, :]

        losses, grads = lax.map(one_block, (ids_row, lens_row, own_row))
        return losses.reshape(U_ROW), grads.reshape(U_ROW, NT, E)

    losses, grads = lax.map(one_row, jnp.arange(N_BATCH, dtype=jnp.int32))
    return losses.reshape(USERS), grads.reshape(USERS, NT, E)
```

```python
import functools
import math

import jax
import jax.numpy as jnp
from jax import lax
from jax.experimental import pallas as pl
from jax.experimental.pallas import tpu as pltpu
from jax.sharding import PartitionSpec as P

MOST = 8
LANES = 128
LQ_ROWS = 16
VMEM_BYTES = 52 << 20
CONTRACT = (((1,), (1,)), ((), ()))
LOG2E = math.log2(math.e)
LN2 = math.log(2.0)


def whole(shape):
    return pl.BlockSpec(shape, lambda *_: (0,) * len(shape))


def pool_kernel(bag, ids_ref, table_ref, out_ref, wide, rows):
    table_rows = table_ref.shape[0]
    unroll = 16

    @pl.when(pl.program_id(0) == 0)
    def _():
        def widen(i, carry):
            at = pl.ds(pl.multiple_of(i * 256, 256), 256)
            wide[at, :] = table_ref[at, :].astype(jnp.float32)
            return carry

        lax.fori_loop(0, table_rows // 256, widen, 0)
        wide[pl.ds(table_rows, 8), :] = jnp.zeros((8, LANES), jnp.float32)

    def group(g, carry):
        base = pl.multiple_of(g * unroll, unroll)
        for j in range(unroll):
            got = [wide[pl.ds(ids_ref[base + (k * LANES + j)], 1), :] for k in range(bag)]
            while len(got) > 1:
                got = [got[i] + got[i + 1] for i in range(0, len(got), 2)]
            rows[pl.ds(base + j, 1), :] = got[0]
        return carry

    lax.fori_loop(0, LANES // unroll, group, 0)
    out_ref[...] = rows[...].astype(jnp.bfloat16)


def pool(ids, table, bag):
    bags = ids.shape[0] // bag
    table_rows, emb = table.shape
    return pl.pallas_call(
        functools.partial(pool_kernel, bag),
        grid=(bags // LANES,),
        in_specs=[
            pl.BlockSpec((LANES * bag,), lambda c: (c,), memory_space=pltpu.SMEM),
            pl.BlockSpec((table_rows, emb), lambda c: (0, 0), pipeline_mode=pl.Buffered(1)),
        ],
        out_specs=pl.BlockSpec((LANES, emb), lambda c: (c, 0)),
        out_shape=jax.ShapeDtypeStruct((bags, emb), jnp.bfloat16),
        scratch_shapes=[
            pltpu.VMEM((table_rows + 8, emb), jnp.float32),
            pltpu.VMEM((LANES, emb), jnp.float32),
        ],
        compiler_params=pltpu.CompilerParams(vmem_limit_bytes=VMEM_BYTES),
        cost_estimate=pl.CostEstimate(
            flops=bags * bag * emb, bytes_accessed=100_000_000, transcendentals=0
        ),
        name="pool",
    )(ids, table)


def items_kernel(ids_ref, row_ref, bank_ref, lq_ref, out_ref, low, high, part_low, part_high):
    count = ids_ref.shape[0]
    owned, width = bank_ref.shape
    items, blocks = lq_ref.shape
    unroll = 16
    step = 256

    def widen(i, carry):
        at = pl.ds(pl.multiple_of(i * step, step), step)
        both = bank_ref[at, :].astype(jnp.float32)
        low[at, :] = both[:, :LANES]
        high[at, :] = both[:, LANES:]
        return carry

    lax.fori_loop(0, owned // step, widen, 0)
    low[pl.ds(owned, 8), :] = jnp.zeros((8, LANES), jnp.float32)
    high[pl.ds(owned, 8), :] = jnp.zeros((8, LANES), jnp.float32)

    def part(c, carry):
        def group(g, inner):
            base = pl.multiple_of(g * unroll, unroll)
            for j in range(unroll):
                at = ids_ref[c * step + base + j]
                part_low[pl.ds(base + j, 1), :] = low[pl.ds(at, 1), :]
                part_high[pl.ds(base + j, 1), :] = high[pl.ds(at, 1), :]
            return inner

        lax.fori_loop(0, step // unroll, group, 0)
        at = pl.ds(pl.multiple_of(c * step, step), step)
        out_ref[at, :] = jnp.concatenate([part_low[...], part_high[...]], axis=1).astype(jnp.bfloat16)
        return carry

    lax.fori_loop(0, count // step, part, 0)
    for c in range(count // step):
        ids = row_ref[:, c * step : (c + 1) * step]
        spot = lax.broadcasted_iota(jnp.int32, (blocks, step), 0)
        one_hot = jnp.where(spot == lax.shift_right_arithmetic(ids, jnp.int32(items.bit_length() - 1)), 1.0, 0.0)
        by_item = jnp.dot(lq_ref[...], one_hot.astype(jnp.bfloat16), preferred_element_type=jnp.float32)
        spot = lax.broadcasted_iota(jnp.int32, (items, step), 0)
        kept = jnp.where(spot == (ids & (items - 1)), by_item, 0.0)
        line = jnp.sum(kept, axis=0, keepdims=True)
        low[pl.ds(c, 1), :] = line[:, :LANES]
        high[pl.ds(c, 1), :] = line[:, LANES:]
    tail = count // step
    out_ref[pl.ds(count, tail), :] = jnp.concatenate(
        [low[pl.ds(0, tail), :], high[pl.ds(0, tail), :]], axis=1
    ).astype(jnp.bfloat16)


def held_items(ids, bank, log_q):
    count = ids.shape[0]
    owned, width = bank.shape
    held = (ids >= 0) & (ids < owned)
    return pl.pallas_call(
        items_kernel,
        in_specs=[
            pl.BlockSpec(memory_space=pltpu.SMEM),
            pl.BlockSpec(memory_space=pltpu.VMEM),
            pl.BlockSpec(memory_space=pltpu.VMEM),
            pl.BlockSpec(memory_space=pltpu.VMEM),
        ],
        out_specs=pl.BlockSpec(memory_space=pltpu.VMEM),
        out_shape=jax.ShapeDtypeStruct((count + count // width, width), jnp.bfloat16),
        scratch_shapes=[
            pltpu.VMEM((owned + 8, LANES), jnp.float32),
            pltpu.VMEM((owned + 8, LANES), jnp.float32),
            pltpu.VMEM((256, LANES), jnp.float32),
            pltpu.VMEM((256, LANES), jnp.float32),
        ],
        compiler_params=pltpu.CompilerParams(vmem_limit_bytes=VMEM_BYTES),
        cost_estimate=pl.CostEstimate(flops=0, bytes_accessed=30_000_000, transcendentals=0),
        name="held_items",
    )(jnp.where(held, ids, owned), ids[None, :], bank, log_q.T)


def tower_kernel(
    scale, lead, slot_ref, npos_ref, own_ref, *refs
):
    (
        *x_refs, w_ref, b_ref, w2_ref, pos_ref, noise_ref, pos_bias_ref, noise_bias_ref,
        grad_ref, loss_ref, pre_ref, score_ref, noise_vec,
    ) = refs
    per_owner = len(x_refs)
    owners, users, emb = x_refs[0].shape
    npos = pos_bias_ref.shape[1]
    nnoise = noise_bias_ref.shape[1]
    items = nnoise // npos_ref.shape[0]
    width = pos_ref.shape[1]
    most = MOST * items

    def weight(s):
        return jnp.concatenate(
            [
                w_ref[pl.ds(pl.multiple_of(slot_ref[s * per_owner + j] * emb, emb), emb), :]
                for j in range(per_owner)
            ],
            axis=0,
        )

    pre = jnp.broadcast_to(b_ref[...], pre_ref.shape)
    for s in range(owners):
        x = jnp.concatenate([r[s] for r in x_refs], axis=1)
        pre = pre + jnp.dot(x, weight(s), preferred_element_type=jnp.float32)
    pre_ref[...] = pre
    hidden = (pre * jax.nn.sigmoid(pre)).astype(jnp.bfloat16)
    user_vec = jnp.dot(hidden, w2_ref[...], preferred_element_type=jnp.float32).astype(jnp.bfloat16)

    def fill(n, carry):
        place = npos_ref[n]
        owner, rank = place // MOST, place % MOST
        start = pl.multiple_of(owner * (most + LQ_ROWS) + rank * items, 16)
        noise_vec[pl.ds(pl.multiple_of(n * items, items), items), :] = noise_ref[pl.ds(start, items), :]
        return carry

    lax.fori_loop(0, npos_ref.shape[0], fill, 0)
    tile = 512
    spans = [(pos_ref, pos_bias_ref, c, c) for c in range(0, npos, tile)]
    spans += [(noise_vec, noise_bias_ref, c, npos + c) for c in range(0, nnoise, tile)]
    top = None
    for vec, bias, c, at in spans:
        s = lax.dot_general(user_vec, vec[c : c + tile, :], CONTRACT, preferred_element_type=jnp.float32)
        s = (s * scale - bias[:, c : c + tile]) * LOG2E
        score_ref[:, at : at + tile] = s
        for k in range(0, tile, LANES):
            piece = s[:, k : k + LANES]
            top = piece if top is None else jnp.maximum(top, piece)
    top = jnp.max(top, axis=1, keepdims=True)
    mixed = jnp.zeros((users, width), jnp.float32)
    denom = jnp.zeros((users, LANES), jnp.float32)
    for vec, bias, c, at in spans:
        p = jnp.exp2(score_ref[:, at : at + tile] - top)
        for k in range(0, tile, LANES):
            denom = denom + p[:, k : k + LANES]
        mixed = mixed + jnp.dot(p.astype(jnp.bfloat16), vec[c : c + tile, :], preferred_element_type=jnp.float32)
    denom = jnp.sum(denom, axis=1, keepdims=True)
    own = pos_ref[pl.ds(pl.multiple_of(own_ref[0] + lead, 16), users), :].astype(jnp.float32)
    own_dot = jnp.sum(user_vec.astype(jnp.float32) * own, axis=1, keepdims=True) * scale
    loss_ref[...] = (top + jnp.log2(denom)) * LN2 - own_dot
    user_grad = ((mixed / denom - own) * scale).astype(jnp.bfloat16)
    hidden_grad = lax.dot_general(user_grad, w2_ref[...], CONTRACT, preferred_element_type=jnp.float32)
    pre = pre_ref[...]
    sig = jax.nn.sigmoid(pre)
    pre_grad = (hidden_grad * sig * (1.0 + pre * (1.0 - sig))).astype(jnp.bfloat16)
    for s in range(owners):
        grad_ref[s] = lax.dot_general(
            pre_grad, weight(s), CONTRACT, preferred_element_type=jnp.float32
        ).astype(jnp.bfloat16)


def tower(part, users, slot, npos, own, xs, w, b, w2, pos, noise, pos_bias, noise_bias):
    owners, _, emb = xs[0].shape
    per_owner = len(xs)
    hid, width = w2.shape
    candidates = pos_bias.shape[1] + noise_bias.shape[1]
    once = pl.Buffered(1)
    smem = pl.BlockSpec(memory_space=pltpu.SMEM)
    flops = 2 * users * (2 * w.shape[0] * hid + 2 * hid * width + 2 * candidates * width)
    return pl.pallas_call(
        functools.partial(tower_kernel, width ** (-0.5), part * users),
        grid=(1,),
        in_specs=[smem] * 3
        + [pl.BlockSpec((owners, users, emb), lambda i: (0, part, 0), pipeline_mode=once)] * per_owner
        + [
            pl.BlockSpec(a.shape, lambda i: (0, 0), pipeline_mode=once)
            for a in (w, b, w2, pos, noise, pos_bias, noise_bias)
        ],
        out_specs=[
            pl.BlockSpec((owners, users, per_owner * emb), lambda i: (0, 0, 0)),
            pl.BlockSpec((users, 1), lambda i: (0, 0)),
        ],
        out_shape=[
            jax.ShapeDtypeStruct((owners, users, per_owner * emb), jnp.bfloat16),
            jax.ShapeDtypeStruct((users, 1), jnp.float32),
        ],
        scratch_shapes=[
            pltpu.VMEM((users, hid), jnp.float32),
            pltpu.VMEM((users, candidates), jnp.float32),
            pltpu.VMEM((noise_bias.shape[1], width), jnp.bfloat16),
        ],
        compiler_params=pltpu.CompilerParams(vmem_limit_bytes=VMEM_BYTES),
        cost_estimate=pl.CostEstimate(
            flops=flops, bytes_accessed=30_000_000, transcendentals=users * candidates
        ),
        name="tower",
    )(slot, npos, own, *xs, w, b, w2, pos, noise, pos_bias, noise_bias)


def on_device(
    tables,
    feature_ids,
    bag_lengths,
    feature_slot,
    w_first,
    b_first,
    w_second,
    bank,
    log_q,
    noise_lists,
    pos_items,
):
    row_users, per_owner, bag = feature_ids.shape
    _, table_rows, emb = tables.shape
    owners = lax.axis_size("table")
    me = lax.axis_index("table")
    blocks_dev, block_items, width = bank.shape
    users = row_users // owners

    item_ids = lax.all_gather(pos_items, "table", axis=0, tiled=True)
    owned = blocks_dev * block_items
    mine = held_items(item_ids - me * owned, bank.reshape(owned, width), log_q)
    pos = lax.psum(mine, "table")
    sample = noise_lists[0]
    owner_of = sample // blocks_dev
    same = owner_of[:, None] == owner_of[None, :]
    index = jnp.arange(sample.shape[0], dtype=jnp.int32)
    rank = jnp.sum((same & (index[None, :] < index[:, None])).astype(jnp.int32), axis=1)
    npos = owner_of * MOST + rank
    pick = (npos[None, :] == (me * MOST + jnp.arange(MOST, dtype=jnp.int32))[:, None]).astype(jnp.int32)
    local_block = jnp.sum(pick * (sample - me * blocks_dev)[None, :], axis=1)
    noise_lq = jnp.pad(log_q[local_block], ((0, LQ_ROWS - MOST), (0, width - block_items)))
    my_noise = jnp.concatenate([bank[local_block].reshape(MOST * block_items, width), noise_lq], axis=0)
    noise = lax.all_gather(my_noise, "table", axis=0, tiled=True)
    w_whole = lax.all_gather(w_first, "batch", axis=0, tiled=True)

    by_table = jnp.transpose(feature_ids, (1, 2, 0))
    used = jnp.arange(bag, dtype=jnp.int32)[None, :, None] < jnp.transpose(bag_lengths, (1, 0))[:, None, :]
    by_table = jnp.where(used, by_table, table_rows)
    by_table = by_table.reshape(per_owner, bag, row_users // LANES, LANES)
    flat_ids = jnp.transpose(by_table, (0, 2, 1, 3)).reshape(per_owner, row_users * bag)
    xs = []
    for j in range(per_owner):
        pooled = pool(flat_ids[j], tables[j], bag).reshape(owners, users, emb)
        xs.append(lax.all_to_all(pooled, "table", split_axis=0, concat_axis=0, tiled=True))

    pos_bias = pos[row_users:].astype(jnp.float32).reshape(1, row_users)
    by_owner = noise.reshape(owners, MOST * block_items + LQ_ROWS, width)
    got_lq = by_owner[:, MOST * block_items : MOST * block_items + MOST, :block_items]
    got_lq = got_lq.reshape(owners * MOST, block_items).astype(jnp.float32)
    noise_bias = got_lq[npos].reshape(1, -1)
    own = (me * users).astype(jnp.int32)[None]
    parts = 2
    grads, losses = [], []
    for part in range(parts):
        grad, loss = tower(
            part, users // parts, feature_slot, npos, own, xs, w_whole, b_first[None, :], w_second,
            pos, noise, pos_bias, noise_bias,
        )
        grads.append(lax.all_to_all(grad, "table", split_axis=0, concat_axis=0, tiled=True))
        losses.append(loss[:, 0])
    own_lq = lax.dynamic_slice_in_dim(pos_bias[0], me * users, users, 0)
    loss = jnp.concatenate(losses) + own_lq
    grad = jnp.concatenate(grads, axis=1).reshape(row_users, per_owner, emb)
    return (loss, grad)


def solution(mesh):
    return jax.shard_map(
        on_device,
        mesh=mesh,
        in_specs=(
            P("table", None, None),
            P("batch", "table", None),
            P("batch", "table"),
            P(),
            P("batch", None),
            P(),
            P(),
            P("table", None, None),
            P("table", None),
            P("batch", None),
            P(("batch", "table")),
        ),
        out_specs=(P(("batch", "table")), P("batch", "table", None)),
        check_vma=False,
    )
```

```python
import functools
import math

import jax
import jax.numpy as jnp
from jax import lax
from jax.experimental import pallas as pl
from jax.experimental.pallas import tpu as pltpu
from jax.sharding import PartitionSpec as P

MOST = 8
LANES = 128
LQ_ROWS = 16
VMEM_BYTES = 52 << 20
ITEM_BYTES = 24 << 20
CONTRACT = (((1,), (1,)), ((), ()))
LOG2E = math.log2(math.e)
LN2 = math.log(2.0)


def whole(shape):
    return pl.BlockSpec(shape, lambda *_: (0,) * len(shape))


def pool_kernel(bag, ids_ref, table_ref, *refs):
    out_ref, wide, rows = refs[-3:]
    table_rows = table_ref.shape[1]
    unroll = 16

    @pl.when(pl.program_id(0) == 0)
    def _():
        def widen(i, carry):
            at = pl.ds(pl.multiple_of(i * 256, 256), 256)
            wide[at, :] = table_ref[0, at, :].astype(jnp.float32)
            return carry

        lax.fori_loop(0, table_rows // 256, widen, 0)
        wide[pl.ds(table_rows, 8), :] = jnp.zeros((8, LANES), jnp.float32)

    def group(g, carry):
        base = pl.multiple_of(g * unroll, unroll)
        for j in range(unroll):
            got = [wide[pl.ds(ids_ref[base + (k * LANES + j)], 1), :] for k in range(bag)]
            while len(got) > 1:
                got = [got[i] + got[i + 1] for i in range(0, len(got), 2)]
            rows[pl.ds(base + j, 1), :] = got[0]
        return carry

    lax.fori_loop(0, LANES // unroll, group, 0)
    out_ref[...] = rows[...].astype(jnp.bfloat16)


def pool(ids, tables, table, bag, order, first, last, blocks, given):
    _, table_rows, emb = tables.shape
    more = [] if given is None else [given]
    return pl.pallas_call(
        functools.partial(pool_kernel, bag),
        grid=(last - first,),
        in_specs=[
            pl.BlockSpec((LANES * bag,), lambda c: (order(c + first),), memory_space=pltpu.SMEM),
            pl.BlockSpec((1, table_rows, emb), lambda c: (table, 0, 0), pipeline_mode=pl.Buffered(1)),
        ]
        + [pl.BlockSpec(memory_space=pl.ANY)] * len(more),
        out_specs=pl.BlockSpec((LANES, emb), lambda c: (c + first, 0)),
        out_shape=jax.ShapeDtypeStruct((blocks * LANES, emb), jnp.bfloat16),
        scratch_shapes=[
            pltpu.VMEM((table_rows + 8, emb), jnp.float32),
            pltpu.VMEM((LANES, emb), jnp.float32),
        ],
        input_output_aliases={2: 0} if more else {},
        compiler_params=pltpu.CompilerParams(vmem_limit_bytes=VMEM_BYTES),
        cost_estimate=pl.CostEstimate(
            flops=(last - first) * LANES * bag * emb,
            bytes_accessed=(last - first) * 100_000,
            transcendentals=0,
        ),
        name="pool",
    )(ids, tables, *more)


def items_kernel(users, place_ref, ids_ref, row_ref, bank_ref, lq_ref, *refs):
    *out_refs, low, high, part_low, part_high = refs
    count = ids_ref.shape[0]
    owned, width = bank_ref.shape
    items, blocks = lq_ref.shape
    unroll = 16
    step = 256

    def widen(i, carry):
        at = pl.ds(pl.multiple_of(i * step, step), step)
        both = bank_ref[at, :].astype(jnp.float32)
        low[at, :] = both[:, :LANES]
        high[at, :] = both[:, LANES:]
        return carry

    lax.fori_loop(0, owned // step, widen, 0)
    low[pl.ds(owned, 8), :] = jnp.zeros((8, LANES), jnp.float32)
    high[pl.ds(owned, 8), :] = jnp.zeros((8, LANES), jnp.float32)
    per = users // step
    held = users + LQ_ROWS
    me = place_ref[0]
    for p, out_ref in enumerate(out_refs):
        def part(c, carry):
            block = c // per
            start = (me ^ (2 * block + p)) * users + (c % per) * step

            def group(g, inner):
                base = pl.multiple_of(g * unroll, unroll)
                for j in range(unroll):
                    at = ids_ref[start + base + j]
                    part_low[pl.ds(base + j, 1), :] = low[pl.ds(at, 1), :]
                    part_high[pl.ds(base + j, 1), :] = high[pl.ds(at, 1), :]
                return inner

            lax.fori_loop(0, step // unroll, group, 0)
            at = pl.ds(pl.multiple_of((c % per) * step, 16), step)
            out_ref[block, at, :] = jnp.concatenate([part_low[...], part_high[...]], axis=1).astype(jnp.bfloat16)
            return carry

        lax.fori_loop(0, count // step // 2, part, 0)
        for block in range(out_ref.shape[0]):
            lines = []
            for c in range(per):
                at = pl.multiple_of((me ^ (2 * block + p)) * users + c * step, step)
                ids = row_ref[:, pl.ds(at, step)]
                spot = lax.broadcasted_iota(jnp.int32, (blocks, step), 0)
                shift = jnp.int32(items.bit_length() - 1)
                one_hot = jnp.where(spot == lax.shift_right_arithmetic(ids, shift), 1.0, 0.0)
                by_item = jnp.dot(lq_ref[...], one_hot.astype(jnp.bfloat16), preferred_element_type=jnp.float32)
                spot = lax.broadcasted_iota(jnp.int32, (items, step), 0)
                kept = jnp.where(spot == (ids & (items - 1)), by_item, 0.0)
                lines.append(jnp.sum(kept, axis=0, keepdims=True))
            lines.append(jnp.zeros((LQ_ROWS - per, step), jnp.float32))
            out_ref[block, pl.ds(users, LQ_ROWS), :] = jnp.concatenate(lines, axis=0).astype(jnp.bfloat16)


def held_items(place, ids, users, bank, log_q):
    count = ids.shape[0]
    owned, width = bank.shape
    held = (ids >= 0) & (ids < owned)
    out = jax.ShapeDtypeStruct((count // users // 2, users + LQ_ROWS, width), jnp.bfloat16)
    return pl.pallas_call(
        functools.partial(items_kernel, users),
        in_specs=[pl.BlockSpec(memory_space=pltpu.SMEM)] * 2 + [pl.BlockSpec(memory_space=pltpu.VMEM)] * 3,
        out_specs=[pl.BlockSpec(memory_space=pltpu.VMEM)] * 2,
        out_shape=[out, out],
        scratch_shapes=[
            pltpu.VMEM((owned + 8, LANES), jnp.float32),
            pltpu.VMEM((owned + 8, LANES), jnp.float32),
            pltpu.VMEM((256, LANES), jnp.float32),
            pltpu.VMEM((256, LANES), jnp.float32),
        ],
        compiler_params=pltpu.CompilerParams(vmem_limit_bytes=ITEM_BYTES),
        cost_estimate=pl.CostEstimate(flops=0, bytes_accessed=30_000_000, transcendentals=0),
        name="held_items",
    )(place, jnp.where(held, ids, owned), ids[None, :], bank, log_q.T)


def tower_kernel(scale, lead, n_x, table_of_ref, count_ref, *refs):
    x_refs, refs = refs[:n_x], refs[n_x:]
    owners, users, emb = x_refs[0].shape
    w_first_ref, b_ref, w2_ref, *refs = refs
    pos_refs, refs = refs[:owners], refs[owners:]
    noise_refs, refs = refs[:2], refs[2:]
    grad_ref, loss_ref, w_ref, pre_ref, score_ref, noise_vec, noise_lq, picked_lq, w_sem = refs
    depth = n_x * emb
    held, width = pos_refs[0].shape
    batch_users = held - LQ_ROWS
    most = 2 * noise_refs[0].shape[0] // owners - LQ_ROWS
    items = most // MOST
    nnoise = noise_vec.shape[0]

    def place(slot, table):
        return pltpu.make_async_copy(
            w_first_ref.at[pl.ds(slot * emb, emb), :],
            w_ref.at[pl.ds(pl.multiple_of(table * emb, emb), emb), :],
            w_sem.at[table],
        )

    for slot in range(w_first_ref.shape[0] // emb):
        place(slot, table_of_ref[slot]).start()
    filled = jnp.int32(0)
    for o in range(owners):
        noise_ref = noise_refs[o // (owners // 2)]
        begin = o % (owners // 2) * (most + LQ_ROWS)
        noise_lq[...] = noise_ref[pl.ds(begin + most, LQ_ROWS), :LANES].astype(jnp.float32)
        used = count_ref[o]

        def fill(k, carry):
            n = filled + k
            start = pl.multiple_of(begin + k * items, 16)
            noise_vec[pl.ds(pl.multiple_of(n * items, items), items), :] = noise_ref[pl.ds(start, items), :]
            picked_lq[pl.ds(n, 1), :] = noise_lq[pl.ds(k, 1), :]
            return carry

        lax.fori_loop(0, used, fill, 0)
        filled = filled + used
    def weight(s):
        return w_ref[pl.ds(pl.multiple_of(s * depth, depth), depth), :]

    pre = jnp.broadcast_to(b_ref[...], pre_ref.shape)
    for s in range(owners):
        x = jnp.concatenate([r[s] for r in x_refs], axis=1)
        for table in range(s * n_x, (s + 1) * n_x):
            place(0, table).wait()
        pre = pre + jnp.dot(x, weight(s), preferred_element_type=jnp.float32)
    pre_ref[...] = pre
    hidden = (pre * jax.nn.sigmoid(pre)).astype(jnp.bfloat16)
    user_vec = jnp.dot(hidden, w2_ref[...], preferred_element_type=jnp.float32).astype(jnp.bfloat16)
    tile = 512
    spans = []
    for ref in pos_refs:
        lines = ref[pl.ds(batch_users, LQ_ROWS), :].astype(jnp.float32)
        line = jnp.concatenate([lines[i : i + 1, :] for i in range(batch_users // width)], axis=1)
        for c in range(0, batch_users, tile):
            spans.append((ref, c, line[:, c : c + tile]))
    for c in range(0, nnoise, tile):
        rows = [picked_lq[pl.ds(n, 1), :][:, :items] for n in range(c // items, (c + tile) // items)]
        spans.append((noise_vec, c, jnp.concatenate(rows, axis=1)))
    top = None
    for n, (vec, c, bias) in enumerate(spans):
        s = lax.dot_general(user_vec, vec[pl.ds(c, tile), :], CONTRACT, preferred_element_type=jnp.float32)
        s = (s * scale - bias) * LOG2E
        score_ref[:, n * tile : (n + 1) * tile] = s
        for k in range(0, tile, LANES):
            piece = s[:, k : k + LANES]
            top = piece if top is None else jnp.maximum(top, piece)
    top = jnp.max(top, axis=1, keepdims=True)
    mixed = jnp.zeros((users, width), jnp.float32)
    denom = jnp.zeros((users, LANES), jnp.float32)
    for n, (vec, c, _) in enumerate(spans):
        p = jnp.exp2(score_ref[:, n * tile : (n + 1) * tile] - top)
        for k in range(0, tile, LANES):
            denom = denom + p[:, k : k + LANES]
        mixed = mixed + jnp.dot(p.astype(jnp.bfloat16), vec[pl.ds(c, tile), :], preferred_element_type=jnp.float32)
    denom = jnp.sum(denom, axis=1, keepdims=True)
    own = pos_refs[0][pl.ds(lead, users), :].astype(jnp.float32)
    own_dot = jnp.sum(user_vec.astype(jnp.float32) * own, axis=1, keepdims=True) * scale
    loss_ref[...] = (top + jnp.log2(denom)) * LN2 - own_dot
    user_grad = ((mixed / denom - own) * scale).astype(jnp.bfloat16)
    hidden_grad = lax.dot_general(user_grad, w2_ref[...], CONTRACT, preferred_element_type=jnp.float32)
    pre = pre_ref[...]
    sig = jax.nn.sigmoid(pre)
    pre_grad = (hidden_grad * sig * (1.0 + pre * (1.0 - sig))).astype(jnp.bfloat16)
    for s in range(owners):
        grad_ref[s] = lax.dot_general(
            pre_grad, weight(s), CONTRACT, preferred_element_type=jnp.float32
        ).astype(jnp.bfloat16)


def tower(lead, users, table_of, counts, xs, w, b, w2, pos, noise, n_noise):
    owners, _, emb = xs[0][0].shape
    per_owner = len(xs)
    hid, width = w2.shape
    depth = owners * per_owner * emb
    candidates = owners * (pos[0].shape[0] - LQ_ROWS) + n_noise
    once = pl.Buffered(1)
    smem = pl.BlockSpec(memory_space=pltpu.SMEM)
    flops = 2 * users * (2 * depth * hid + 2 * hid * width + 2 * candidates * width)
    wide = per_owner * emb
    return pl.pallas_call(
        functools.partial(tower_kernel, width ** (-0.5), lead, per_owner),
        grid=(1,),
        in_specs=[smem] * 2
        + [
            pl.BlockSpec((owners, users, emb), lambda i, at=at: (0, at, 0), pipeline_mode=once) for _, at in xs
        ]
        + [pl.BlockSpec(memory_space=pl.ANY)]
        + [pl.BlockSpec(a.shape, lambda i: (0, 0), pipeline_mode=once) for a in (b, w2, *pos, *noise)],
        out_specs=[
            pl.BlockSpec((owners, users, wide), lambda i: (0, 0, 0)),
            pl.BlockSpec((users, 1), lambda i: (0, 0)),
        ],
        out_shape=[
            jax.ShapeDtypeStruct((owners, users, wide), jnp.bfloat16),
            jax.ShapeDtypeStruct((users, 1), jnp.float32),
        ],
        scratch_shapes=[
            pltpu.VMEM((depth, hid), jnp.bfloat16),
            pltpu.VMEM((users, hid), jnp.float32),
            pltpu.VMEM((users, candidates), jnp.float32),
            pltpu.VMEM((n_noise, width), jnp.bfloat16),
            pltpu.VMEM((LQ_ROWS, LANES), jnp.float32),
            pltpu.VMEM((n_noise * MOST // (2 * noise[0].shape[0] // owners - LQ_ROWS), LANES), jnp.float32),
            pltpu.SemaphoreType.DMA((depth // emb,)),
        ],
        compiler_params=pltpu.CompilerParams(vmem_limit_bytes=VMEM_BYTES),
        cost_estimate=pl.CostEstimate(
            flops=flops, bytes_accessed=60_000_000, transcendentals=users * candidates
        ),
        name="tower",
    )(table_of, counts, *(x for x, _ in xs), w, b, w2, *pos, *noise)


def swap(x, axis, offset):
    size = lax.axis_size(axis)
    return lax.ppermute(x, axis, [(i, i ^ offset) for i in range(size)])


class Spread:
    def __init__(self, x, axis):
        self.axis, self.size = axis, lax.axis_size(axis)
        self.offset = self.size // 2
        self.got, self.fresh, self.sent = {0: x}, [0], {}

    def send(self, tied=()):
        self.got.update(zip(self.sent, tied))
        sent = {}
        if self.offset > 1:
            sent = {o | self.offset: swap(v, self.axis, self.offset) for o, v in self.got.items() if not o & 1}
        sent.update({o | 1: swap(self.got[o], self.axis, 1) for o in self.fresh})
        self.fresh = [o for o in sent if not o & 1]
        self.offset //= 2
        self.sent = sent
        return list(sent.values())

    def finish(self, tied=()):
        values = self.send(tied)
        while self.sent:
            values = self.send(values)
        return [self.got[o] for o in range(self.size)]


def tie(*values):
    return lax.optimization_barrier(values)


def on_device(
    tables,
    feature_ids,
    bag_lengths,
    feature_slot,
    w_first,
    b_first,
    w_second,
    bank,
    log_q,
    noise_lists,
    pos_items,
):
    row_users, per_owner, bag = feature_ids.shape
    _, table_rows, emb = tables.shape
    owners = lax.axis_size("table")
    me = lax.axis_index("table")
    blocks_dev, block_items, width = bank.shape
    users = row_users // owners

    place = me.astype(jnp.int32)[None]

    copies = jnp.broadcast_to(pos_items[None, :], (owners, users))
    item_ids = lax.all_to_all(copies, "table", split_axis=0, concat_axis=0, tiled=True).reshape(-1)
    sample = noise_lists[0]
    owner_of = sample // blocks_dev
    same = owner_of[:, None] == owner_of[None, :]
    index = jnp.arange(sample.shape[0], dtype=jnp.int32)
    rank = jnp.sum((same & (index[None, :] < index[:, None])).astype(jnp.int32), axis=1)
    npos = owner_of * MOST + rank
    pick = (npos[None, :] == (me * MOST + jnp.arange(MOST, dtype=jnp.int32))[:, None]).astype(jnp.int32)
    local_block = jnp.sum(pick * (sample - me * blocks_dev)[None, :], axis=1)
    noise_lq = jnp.pad(log_q[local_block], ((0, LQ_ROWS - MOST), (0, width - block_items)))
    my_noise = jnp.concatenate([bank[local_block].reshape(MOST * block_items, width), noise_lq], axis=0)
    w_whole = lax.all_gather(w_first, "batch", axis=0, tiled=True)
    near_noise, noise_from, offset = [my_noise], [0], owners // 2
    noise_got = [swap(my_noise, "table", offset)]
    owned = blocks_dev * block_items
    same, other = held_items(place, item_ids - me * owned, users, bank.reshape(owned, width), log_q)

    by_table = jnp.transpose(feature_ids, (1, 2, 0))
    used = jnp.arange(bag, dtype=jnp.int32)[None, :, None] < jnp.transpose(bag_lengths, (1, 0))[:, None, :]
    by_table = jnp.where(used, by_table, table_rows)
    by_table = by_table.reshape(per_owner, bag, row_users // LANES, LANES)
    by_table = jnp.transpose(by_table, (0, 2, 1, 3)).reshape(per_owner, row_users * bag)
    ids = [by_table[j] for j in range(per_owner)]
    blocks = row_users // LANES
    block_users = users // LANES
    part_blocks = block_users // 2
    half = blocks // 2

    def straight(c):
        return c

    def halves(c):
        h, c = c // half, c % half
        return c // part_blocks * block_users + h * part_blocks + c % part_blocks

    def exchange(pooled):
        pooled = pooled.reshape(owners, -1, emb)
        return lax.all_to_all(pooled, "table", split_axis=0, concat_axis=0, tiled=True)

    def both(a, b):
        return (a.astype(jnp.float32) + b.astype(jnp.float32)).astype(jnp.bfloat16)

    same, other, tables, *ids = tie(same, other, tables, *ids)

    def more_noise():
        near_noise.extend(noise_got)
        noise_from.extend([o ^ offset for o in noise_from])

    near = swap(other, "table", 1)
    while offset > 2:
        more_noise()
        offset //= 2
        noise_got = [swap(v, "table", offset) for v in near_noise]
    cut = blocks * 5 // 8
    pooled = pool(ids[0], tables, 0, bag, straight, 0, cut, blocks, None)
    pooled, near, noise_got, *ids = tie(pooled, near, noise_got, *ids)
    more_noise()
    near_noise = jnp.concatenate(near_noise, axis=0)
    far_noise = swap(near_noise, "table", 1)
    sums = [both(same[q], near[q]) for q in range(owners // 2)]
    far = [swap(sums[q], "table", 2 * q) for q in range(1, owners // 2)]
    pooled = pool(ids[0], tables, 0, bag, straight, cut, blocks, blocks, pooled)
    whole = [pooled]
    for j in range(1, per_owner - 1):
        tables, pooled = tie(tables, pooled)
        pooled = pool(ids[j], tables, j, bag, straight, 0, blocks, blocks, None)
        whole.append(pooled)

    tables, whole, far, sums, far_noise = tie(tables, whole, far, sums, far_noise)
    own_pos = sums[0].astype(jnp.float32)
    for block in far:
        own_pos = own_pos + block.astype(jnp.float32)
    own_pos = own_pos.astype(jnp.bfloat16)
    own_pos, tables = tie(own_pos, tables)
    pos_rounds = Spread(own_pos, "table")
    got = pos_rounds.send()

    last = ids[-1]
    final = functools.partial(pool, tables=tables, table=per_owner - 1, bag=bag, order=halves, blocks=blocks)
    cut = blocks // 4
    pooled = final(ids=last, first=0, last=cut, given=None)
    pooled, whole, got, last = tie(pooled, whole, got, last)
    xs = [exchange(v) for v in whole]
    got = pos_rounds.send(got)
    pooled = final(ids=last, first=cut, last=blocks - cut, given=pooled)
    pooled, xs, got, last = tie(pooled, xs, got, last)
    early = exchange(pooled[: row_users // 2])
    got = pos_rounds.send(got)
    pooled = final(ids=last, first=blocks - cut, last=blocks, given=pooled)
    pooled, early, got = tie(pooled, early, got)
    late = exchange(pooled[row_users // 2 :])
    pos = pos_rounds.finish(got)

    slots = jnp.arange(feature_slot.shape[0], dtype=jnp.int32)
    table_of = jnp.sum(jnp.where(feature_slot[None, :] == slots[:, None], slots[None, :], 0), axis=1)
    noise_owner = me ^ jnp.asarray(noise_from + [o ^ 1 for o in noise_from], jnp.int32)
    counts = jnp.sum((owner_of[None, :] == noise_owner[:, None]).astype(jnp.int32), axis=1)
    run = functools.partial(
        tower, users=users // 2, table_of=table_of, counts=counts, w=w_whole, b=b_first[None, :], w2=w_second, pos=pos,
        noise=[near_noise, far_noise], n_noise=sample.shape[0] * block_items,
    )
    grad_early, loss_early = run(lead=0, xs=[(v, 0) for v in xs] + [(early, 0)])
    back = [lax.all_to_all(grad_early, "table", split_axis=0, concat_axis=0, tiled=True)]
    _, late = tie(loss_early, late)
    grad_late, loss_late = run(lead=users // 2, xs=[(v, 1) for v in xs] + [(late, 0)])
    back[0], grad_late = tie(back[0], grad_late)
    back.append(lax.all_to_all(grad_late, "table", split_axis=0, concat_axis=0, tiled=True))
    losses = [loss_early[:, 0], loss_late[:, 0]]
    own_lq = own_pos[users : users + users // width].astype(jnp.float32).reshape(users)
    grad = jnp.concatenate(back, axis=1).reshape(row_users, per_owner, emb)
    return (jnp.concatenate(losses) + own_lq, grad)


def solution(mesh):
    return jax.shard_map(
        on_device,
        mesh=mesh,
        in_specs=(
            P("table", None, None),
            P("batch", "table", None),
            P("batch", "table"),
            P(),
            P("batch", None),
            P(),
            P(),
            P("table", None, None),
            P("table", None),
            P("batch", None),
            P(("batch", "table")),
        ),
        out_specs=(P(("batch", "table")), P("batch", "table", None)),
        check_vma=False,
    )
```

```python
import functools
import math

import jax
import jax.numpy as jnp
from jax import lax
from jax.experimental import pallas as pl
from jax.experimental.pallas import tpu as pltpu
from jax.sharding import PartitionSpec as P

MOST = 8
LANES = 128
LQ_ROWS = 16
VMEM_BYTES = 52 << 20
ITEM_BYTES = 24 << 20
CONTRACT = (((1,), (1,)), ((), ()))
LOG2E = math.log2(math.e)
LN2 = math.log(2.0)


def whole(shape):
    return pl.BlockSpec(shape, lambda *_: (0,) * len(shape))


def pool_kernel(bag, ids_ref, table_ref, *refs):
    out_ref, wide, rows = refs[-3:]
    table_rows = table_ref.shape[1]
    unroll = 16

    @pl.when(pl.program_id(0) == 0)
    def _():
        def widen(i, carry):
            at = pl.ds(pl.multiple_of(i * 256, 256), 256)
            wide[at, :] = table_ref[0, at, :].astype(jnp.float32)
            return carry

        lax.fori_loop(0, table_rows // 256, widen, 0)
        wide[pl.ds(table_rows, 8), :] = jnp.zeros((8, LANES), jnp.float32)

    def group(g, carry):
        base = pl.multiple_of(g * unroll, unroll)
        for j in range(unroll):
            got = [wide[pl.ds(ids_ref[base + (k * LANES + j)], 1), :] for k in range(bag)]
            while len(got) > 1:
                got = [got[i] + got[i + 1] for i in range(0, len(got), 2)]
            rows[pl.ds(base + j, 1), :] = got[0]
        return carry

    lax.fori_loop(0, LANES // unroll, group, 0)
    out_ref[...] = rows[...].astype(jnp.bfloat16)


def pool(ids, tables, table, bag, order, first, last, blocks, given):
    _, table_rows, emb = tables.shape
    more = [] if given is None else [given]
    return pl.pallas_call(
        functools.partial(pool_kernel, bag),
        grid=(last - first,),
        in_specs=[
            pl.BlockSpec((LANES * bag,), lambda c: (order(c + first),), memory_space=pltpu.SMEM),
            pl.BlockSpec((1, table_rows, emb), lambda c: (table, 0, 0), pipeline_mode=pl.Buffered(1)),
        ]
        + [pl.BlockSpec(memory_space=pl.ANY)] * len(more),
        out_specs=pl.BlockSpec((LANES, emb), lambda c: (c + first, 0)),
        out_shape=jax.ShapeDtypeStruct((blocks * LANES, emb), jnp.bfloat16),
        scratch_shapes=[
            pltpu.VMEM((table_rows + 8, emb), jnp.float32),
            pltpu.VMEM((LANES, emb), jnp.float32),
        ],
        input_output_aliases={2: 0} if more else {},
        compiler_params=pltpu.CompilerParams(vmem_limit_bytes=VMEM_BYTES),
        cost_estimate=pl.CostEstimate(
            flops=(last - first) * LANES * bag * emb,
            bytes_accessed=(last - first) * 100_000,
            transcendentals=0,
        ),
        name="pool",
    )(ids, tables, *more)


def items_kernel(users, ids_ref, row_ref, bank_ref, lq_ref, *refs):
    out_ref, low, high, part_low, part_high = refs
    count = ids_ref.shape[0]
    owned, width = bank_ref.shape
    items, blocks = lq_ref.shape
    unroll = 16
    step = 256

    def widen(i, carry):
        at = pl.ds(pl.multiple_of(i * step, step), step)
        both = bank_ref[at, :].astype(jnp.float32)
        low[at, :] = both[:, :LANES]
        high[at, :] = both[:, LANES:]
        return carry

    lax.fori_loop(0, owned // step, widen, 0)
    low[pl.ds(owned, 8), :] = jnp.zeros((8, LANES), jnp.float32)
    high[pl.ds(owned, 8), :] = jnp.zeros((8, LANES), jnp.float32)
    per = users // step

    def part(c, carry):
        start = c * step

        def group(g, inner):
            base = pl.multiple_of(g * unroll, unroll)
            for j in range(unroll):
                at = ids_ref[start + base + j]
                part_low[pl.ds(base + j, 1), :] = low[pl.ds(at, 1), :]
                part_high[pl.ds(base + j, 1), :] = high[pl.ds(at, 1), :]
            return inner

        lax.fori_loop(0, step // unroll, group, 0)
        at = pl.ds(pl.multiple_of((c % per) * step, 16), step)
        out_ref[c // per, at, :] = jnp.concatenate([part_low[...], part_high[...]], axis=1).astype(jnp.bfloat16)
        return carry

    lax.fori_loop(0, count // step, part, 0)
    for block in range(count // users):
        lines = []
        for c in range(per):
            ids = row_ref[:, pl.ds(block * users + c * step, step)]
            spot = lax.broadcasted_iota(jnp.int32, (blocks, step), 0)
            shift = jnp.int32(items.bit_length() - 1)
            one_hot = jnp.where(spot == lax.shift_right_arithmetic(ids, shift), 1.0, 0.0)
            by_item = jnp.dot(lq_ref[...], one_hot.astype(jnp.bfloat16), preferred_element_type=jnp.float32)
            spot = lax.broadcasted_iota(jnp.int32, (items, step), 0)
            kept = jnp.where(spot == (ids & (items - 1)), by_item, 0.0)
            lines.append(jnp.sum(kept, axis=0, keepdims=True))
        lines.append(jnp.zeros((LQ_ROWS - per, step), jnp.float32))
        out_ref[block, pl.ds(users, LQ_ROWS), :] = jnp.concatenate(lines, axis=0).astype(jnp.bfloat16)


def held_items(ids, users, bank, log_q):
    count = ids.shape[0]
    owned, width = bank.shape
    held = (ids >= 0) & (ids < owned)
    out = jax.ShapeDtypeStruct((count // users, users + LQ_ROWS, width), jnp.bfloat16)
    return pl.pallas_call(
        functools.partial(items_kernel, users),
        in_specs=[pl.BlockSpec(memory_space=pltpu.SMEM)] + [pl.BlockSpec(memory_space=pltpu.VMEM)] * 3,
        out_specs=pl.BlockSpec(memory_space=pltpu.VMEM),
        out_shape=out,
        scratch_shapes=[
            pltpu.VMEM((owned + 8, LANES), jnp.float32),
            pltpu.VMEM((owned + 8, LANES), jnp.float32),
            pltpu.VMEM((256, LANES), jnp.float32),
            pltpu.VMEM((256, LANES), jnp.float32),
        ],
        compiler_params=pltpu.CompilerParams(vmem_limit_bytes=ITEM_BYTES),
        cost_estimate=pl.CostEstimate(flops=0, bytes_accessed=30_000_000, transcendentals=0),
        name="held_items",
    )(jnp.where(held, ids, owned), ids[None, :], bank, log_q.T)


def tower_kernel(scale, lead, n_x, n_w, n_noise, table_of_ref, count_ref, shard_ref, *refs):
    x_refs, refs = refs[:n_x], refs[n_x:]
    owners, users, emb = x_refs[0].shape
    w_refs, refs = refs[:n_w], refs[n_w:]
    b_ref, w2_ref, *refs = refs
    pos_refs, refs = refs[:owners], refs[owners:]
    noise_refs, refs = refs[:n_noise], refs[n_noise:]
    grad_ref, loss_ref, w_ref, pre_ref, score_ref, noise_vec, noise_lq, picked_lq, w_sem = refs
    depth = n_x * emb
    held, width = pos_refs[0].shape
    batch_users = held - LQ_ROWS
    nnoise = noise_vec.shape[0]
    items = nnoise // picked_lq.shape[0]
    most = MOST * items

    def place(o, i, table):
        return pltpu.make_async_copy(
            w_refs[o].at[pl.ds(i * emb, emb), :],
            w_ref.at[pl.ds(pl.multiple_of(table * emb, emb), emb), :],
            w_sem.at[table],
        )

    per = w_refs[0].shape[0] // emb
    for o in range(n_w):
        for i in range(per):
            place(o, i, table_of_ref[(shard_ref[0] ^ o) * per + i]).start()
    filled = jnp.int32(0)
    step = most + LQ_ROWS
    for o, (noise_ref, begin) in enumerate((r, c) for r in noise_refs for c in range(0, r.shape[0], step)):
        noise_lq[...] = noise_ref[pl.ds(begin + most, LQ_ROWS), :LANES].astype(jnp.float32)
        used = count_ref[o]

        def fill(k, carry, noise_ref=noise_ref, begin=begin, filled=filled):
            n = filled + k
            start = pl.multiple_of(begin + k * items, 16)
            noise_vec[pl.ds(pl.multiple_of(n * items, items), items), :] = noise_ref[pl.ds(start, items), :]
            picked_lq[pl.ds(n, 1), :] = noise_lq[pl.ds(k, 1), :]
            return carry

        lax.fori_loop(0, used, fill, 0)
        filled = filled + used
    def weight(s):
        return w_ref[pl.ds(pl.multiple_of(s * depth, depth), depth), :]

    pre = jnp.broadcast_to(b_ref[...], pre_ref.shape)
    for s in range(owners):
        x = jnp.concatenate([r[s] for r in x_refs], axis=1)
        for table in range(s * n_x, (s + 1) * n_x):
            place(0, 0, table).wait()
        pre = pre + jnp.dot(x, weight(s), preferred_element_type=jnp.float32)
    pre_ref[...] = pre
    hidden = (pre * jax.nn.sigmoid(pre)).astype(jnp.bfloat16)
    user_vec = jnp.dot(hidden, w2_ref[...], preferred_element_type=jnp.float32).astype(jnp.bfloat16)
    tile = 512
    spans = []
    for ref in pos_refs:
        lines = ref[pl.ds(batch_users, LQ_ROWS), :].astype(jnp.float32)
        line = jnp.concatenate([lines[i : i + 1, :] for i in range(batch_users // width)], axis=1)
        for c in range(0, batch_users, tile):
            spans.append((ref, c, line[:, c : c + tile]))
    for c in range(0, nnoise, tile):
        rows = [picked_lq[pl.ds(n, 1), :][:, :items] for n in range(c // items, (c + tile) // items)]
        spans.append((noise_vec, c, jnp.concatenate(rows, axis=1)))
    top = None
    for n, (vec, c, bias) in enumerate(spans):
        s = lax.dot_general(user_vec, vec[pl.ds(c, tile), :], CONTRACT, preferred_element_type=jnp.float32)
        s = (s * scale - bias) * LOG2E
        score_ref[:, n * tile : (n + 1) * tile] = s
        for k in range(0, tile, LANES):
            piece = s[:, k : k + LANES]
            top = piece if top is None else jnp.maximum(top, piece)
    top = jnp.max(top, axis=1, keepdims=True)
    mixed = jnp.zeros((users, width), jnp.float32)
    denom = jnp.zeros((users, LANES), jnp.float32)
    for n, (vec, c, _) in enumerate(spans):
        p = jnp.exp2(score_ref[:, n * tile : (n + 1) * tile] - top)
        for k in range(0, tile, LANES):
            denom = denom + p[:, k : k + LANES]
        mixed = mixed + jnp.dot(p.astype(jnp.bfloat16), vec[pl.ds(c, tile), :], preferred_element_type=jnp.float32)
    denom = jnp.sum(denom, axis=1, keepdims=True)
    own = pos_refs[0][pl.ds(lead, users), :].astype(jnp.float32)
    own_dot = jnp.sum(user_vec.astype(jnp.float32) * own, axis=1, keepdims=True) * scale
    loss_ref[...] = (top + jnp.log2(denom)) * LN2 - own_dot
    user_grad = ((mixed / denom - own) * scale).astype(jnp.bfloat16)
    hidden_grad = lax.dot_general(user_grad, w2_ref[...], CONTRACT, preferred_element_type=jnp.float32)
    pre = pre_ref[...]
    sig = jax.nn.sigmoid(pre)
    pre_grad = (hidden_grad * sig * (1.0 + pre * (1.0 - sig))).astype(jnp.bfloat16)
    for s in range(owners):
        grad_ref[s] = lax.dot_general(
            pre_grad, weight(s), CONTRACT, preferred_element_type=jnp.float32
        ).astype(jnp.bfloat16)


def tower(lead, users, table_of, counts, shard, xs, ws, b, w2, pos, noise, n_noise, n_picked):
    owners, _, emb = xs[0][0].shape
    per_owner = len(xs)
    hid, width = w2.shape
    depth = owners * per_owner * emb
    candidates = owners * (pos[0].shape[0] - LQ_ROWS) + n_noise
    once = pl.Buffered(1)
    smem = pl.BlockSpec(memory_space=pltpu.SMEM)
    flops = 2 * users * (2 * depth * hid + 2 * hid * width + 2 * candidates * width)
    wide = per_owner * emb
    return pl.pallas_call(
        functools.partial(tower_kernel, width ** (-0.5), lead, per_owner, len(ws), len(noise)),
        grid=(1,),
        in_specs=[smem] * 3
        + [
            pl.BlockSpec((owners, users, emb), lambda i, at=at: (0, at, 0), pipeline_mode=once) for _, at in xs
        ]
        + [pl.BlockSpec(memory_space=pl.ANY)] * len(ws)
        + [pl.BlockSpec(a.shape, lambda i: (0, 0), pipeline_mode=once) for a in (b, w2, *pos, *noise)],
        out_specs=[
            pl.BlockSpec((owners, users, wide), lambda i: (0, 0, 0)),
            pl.BlockSpec((users, 1), lambda i: (0, 0)),
        ],
        out_shape=[
            jax.ShapeDtypeStruct((owners, users, wide), jnp.bfloat16),
            jax.ShapeDtypeStruct((users, 1), jnp.float32),
        ],
        scratch_shapes=[
            pltpu.VMEM((depth, hid), jnp.bfloat16),
            pltpu.VMEM((users, hid), jnp.float32),
            pltpu.VMEM((users, candidates), jnp.float32),
            pltpu.VMEM((n_noise, width), jnp.bfloat16),
            pltpu.VMEM((LQ_ROWS, LANES), jnp.float32),
            pltpu.VMEM((n_picked, LANES), jnp.float32),
            pltpu.SemaphoreType.DMA((depth // emb,)),
        ],
        compiler_params=pltpu.CompilerParams(vmem_limit_bytes=VMEM_BYTES),
        cost_estimate=pl.CostEstimate(
            flops=flops, bytes_accessed=60_000_000, transcendentals=users * candidates
        ),
        name="tower",
    )(table_of, counts, shard, *(x for x, _ in xs), *ws, b, w2, *pos, *noise)


def swap(x, axis, offset):
    size = lax.axis_size(axis)
    return lax.ppermute(x, axis, [(i, i ^ offset) for i in range(size)])


class Spread:
    def __init__(self, x, axis):
        self.axis, self.size = axis, lax.axis_size(axis)
        self.offset = self.size // 2
        self.got, self.fresh, self.sent = {0: x}, [0], {}

    def send(self, tied=()):
        self.got.update(zip(self.sent, tied))
        sent = {}
        if self.offset > 1:
            sent = {o | self.offset: swap(v, self.axis, self.offset) for o, v in self.got.items() if not o & 1}
        sent.update({o | 1: swap(self.got[o], self.axis, 1) for o in self.fresh})
        self.fresh = [o for o in sent if not o & 1]
        self.offset //= 2
        self.sent = sent
        return list(sent.values())

    def finish(self, tied=()):
        values = self.send(tied)
        while self.sent:
            values = self.send(values)
        return [self.got[o] for o in range(self.size)]


def tie(*values):
    return lax.optimization_barrier(values)


def on_device(
    tables,
    feature_ids,
    bag_lengths,
    feature_slot,
    w_first,
    b_first,
    w_second,
    bank,
    log_q,
    noise_lists,
    pos_items,
):
    row_users, per_owner, bag = feature_ids.shape
    _, table_rows, emb = tables.shape
    owners = lax.axis_size("table")
    me = lax.axis_index("table")
    blocks_dev, block_items, width = bank.shape
    users = row_users // owners

    shard = lax.axis_index("batch").astype(jnp.int32)[None]

    copies = jnp.broadcast_to(pos_items[None, :], (owners, users))
    item_ids = lax.all_to_all(copies, "table", split_axis=0, concat_axis=0, tiled=True).reshape(-1)
    sample = noise_lists[0]
    owner_of = sample // blocks_dev
    same = owner_of[:, None] == owner_of[None, :]
    index = jnp.arange(sample.shape[0], dtype=jnp.int32)
    rank = jnp.sum((same & (index[None, :] < index[:, None])).astype(jnp.int32), axis=1)
    npos = owner_of * MOST + rank
    pick = (npos[None, :] == (me * MOST + jnp.arange(MOST, dtype=jnp.int32))[:, None]).astype(jnp.int32)
    local_block = jnp.sum(pick * (sample - me * blocks_dev)[None, :], axis=1)
    noise_lq = jnp.pad(log_q[local_block], ((0, LQ_ROWS - MOST), (0, width - block_items)))
    my_noise = jnp.concatenate([bank[local_block].reshape(MOST * block_items, width), noise_lq], axis=0)
    item_ids, my_noise, w_part = tie(item_ids, my_noise, w_first)
    w_rounds = Spread(w_part, "batch")
    w_got = w_rounds.send()
    near_noise, noise_from, offset = [my_noise], [0], owners // 2
    noise_got = [swap(my_noise, "table", offset)]
    owned = blocks_dev * block_items
    mine = held_items(item_ids - me * owned, users, bank.reshape(owned, width), log_q)

    by_table = jnp.transpose(feature_ids, (1, 2, 0))
    used = jnp.arange(bag, dtype=jnp.int32)[None, :, None] < jnp.transpose(bag_lengths, (1, 0))[:, None, :]
    by_table = jnp.where(used, by_table, table_rows)
    by_table = by_table.reshape(per_owner, bag, row_users // LANES, LANES)
    by_table = jnp.transpose(by_table, (0, 2, 1, 3)).reshape(per_owner, row_users * bag)
    ids = [by_table[j] for j in range(per_owner)]
    blocks = row_users // LANES
    block_users = users // LANES
    part_blocks = block_users // 2
    half = blocks // 2

    def straight(c):
        return c

    def halves(c):
        h, c = c // half, c % half
        return c // part_blocks * block_users + h * part_blocks + c % part_blocks

    def exchange(pooled):
        pooled = pooled.reshape(owners, -1, emb)
        return lax.all_to_all(pooled, "table", split_axis=0, concat_axis=0, tiled=True)

    mine, tables, noise_got, *ids = tie(mine, tables, noise_got, *ids)

    def more_noise():
        near_noise.extend(noise_got)
        noise_from.extend([o ^ offset for o in noise_from])

    mine = lax.all_to_all(mine, "table", split_axis=0, concat_axis=0, tiled=True)
    while offset > 2:
        more_noise()
        offset //= 2
        noise_got = [swap(v, "table", offset) for v in near_noise]
    first_noise = swap(jnp.concatenate(near_noise, axis=0), "table", 1)
    pooled = pool(ids[0], tables, 0, bag, straight, 0, blocks, blocks, None)
    whole = [pooled]
    for j in range(1, per_owner - 1):
        tables, pooled = tie(tables, pooled)
        pooled = pool(ids[j], tables, j, bag, straight, 0, blocks, blocks, None)
        whole.append(pooled)

    tables, whole, mine, noise_got, first_noise, w_got = tie(tables, whole, mine, noise_got, first_noise, w_got)
    w_got = w_rounds.send(w_got)
    more_noise()
    far_noise = swap(jnp.concatenate(noise_got, axis=0), "table", 1)
    near_noise = jnp.concatenate(near_noise, axis=0)
    own_pos = jnp.sum(mine.astype(jnp.float32), axis=0).astype(jnp.bfloat16)
    own_pos, tables = tie(own_pos, tables)
    pos_rounds = Spread(own_pos, "table")
    got = pos_rounds.send()

    last = ids[-1]
    final = functools.partial(pool, tables=tables, table=per_owner - 1, bag=bag, order=halves, blocks=blocks)
    cut = blocks // 4
    pooled = final(ids=last, first=0, last=cut, given=None)
    pooled, whole, got, far_noise, last = tie(pooled, whole, got, far_noise, last)
    xs = [exchange(v) for v in whole]
    got = pos_rounds.send(got)
    pooled = final(ids=last, first=cut, last=blocks - cut, given=pooled)
    pooled, xs, got, last = tie(pooled, xs, got, last)
    early = exchange(pooled[: row_users // 2])
    got = pos_rounds.send(got)
    pooled = final(ids=last, first=blocks - cut, last=blocks, given=pooled)
    pooled, early, got = tie(pooled, early, got)
    late = exchange(pooled[row_users // 2 :])
    pos = pos_rounds.finish(got)
    ws = w_rounds.finish(w_got)

    slots = jnp.arange(feature_slot.shape[0], dtype=jnp.int32)
    table_of = jnp.sum(jnp.where(feature_slot[None, :] == slots[:, None], slots[None, :], 0), axis=1)
    noise_owner = me ^ jnp.asarray(noise_from + [o ^ 1 for o in noise_from], jnp.int32)
    counts = jnp.sum((owner_of[None, :] == noise_owner[:, None]).astype(jnp.int32), axis=1)
    run = functools.partial(
        tower, users=users // 2, table_of=table_of, counts=counts, shard=shard, ws=ws, b=b_first[None, :], w2=w_second, pos=pos,
        noise=[near_noise, first_noise, far_noise], n_noise=sample.shape[0] * block_items, n_picked=sample.shape[0],
    )
    grad_early, loss_early = run(lead=0, xs=[(v, 0) for v in xs] + [(early, 0)])
    back = [lax.all_to_all(grad_early, "table", split_axis=0, concat_axis=0, tiled=True)]
    _, late = tie(loss_early, late)
    grad_late, loss_late = run(lead=users // 2, xs=[(v, 1) for v in xs] + [(late, 0)])
    back[0], grad_late = tie(back[0], grad_late)
    back.append(lax.all_to_all(grad_late, "table", split_axis=0, concat_axis=0, tiled=True))
    losses = [loss_early[:, 0], loss_late[:, 0]]
    own_lq = own_pos[users : users + users // width].astype(jnp.float32).reshape(users)
    grad = jnp.concatenate(back, axis=1).reshape(row_users, per_owner, emb)
    return (jnp.concatenate(losses) + own_lq, grad)


def solution(mesh):
    return jax.shard_map(
        on_device,
        mesh=mesh,
        in_specs=(
            P("table", None, None),
            P("batch", "table", None),
            P("batch", "table"),
            P(),
            P("batch", None),
            P(),
            P(),
            P("table", None, None),
            P("table", None),
            P("batch", None),
            P(("batch", "table")),
        ),
        out_specs=(P(("batch", "table")), P("batch", "table", None)),
        check_vma=False,
    )
```

```python
import functools
import math

import jax
import jax.numpy as jnp
from jax import lax
from jax.experimental import pallas as pl
from jax.experimental.pallas import tpu as pltpu
from jax.sharding import PartitionSpec as P

MOST = 8
LANES = 128
LQ_ROWS = 16
VMEM_BYTES = 52 << 20
ITEM_BYTES = 24 << 20
CONTRACT = (((1,), (1,)), ((), ()))
LOG2E = math.log2(math.e)
LN2 = math.log(2.0)


def whole(shape):
    return pl.BlockSpec(shape, lambda *_: (0,) * len(shape))


def pool_kernel(bag, ids_ref, table_ref, *refs):
    out_ref, wide, rows = refs[-3:]
    table_rows = table_ref.shape[1]
    unroll = 32

    @pl.when(pl.program_id(0) == 0)
    def _():
        def widen(i, carry):
            at = pl.ds(pl.multiple_of(i * 256, 256), 256)
            wide[at, :] = table_ref[0, at, :].astype(jnp.float32)
            return carry

        lax.fori_loop(0, table_rows // 256, widen, 0)
        wide[pl.ds(table_rows, 8), :] = jnp.zeros((8, LANES), jnp.float32)

    def group(g, carry):
        base = pl.multiple_of(g * unroll, unroll)
        for j in range(unroll):
            got = [wide[pl.ds(ids_ref[base + (k * LANES + j)], 1), :] for k in range(bag)]
            while len(got) > 1:
                got = [got[i] + got[i + 1] for i in range(0, len(got), 2)]
            rows[pl.ds(base + j, 1), :] = got[0]
        return carry

    lax.fori_loop(0, LANES // unroll, group, 0)
    out_ref[...] = rows[...].astype(jnp.bfloat16)


def pool(ids, tables, table, bag, order, first, last, blocks, given):
    _, table_rows, emb = tables.shape
    more = [] if given is None else [given]
    return pl.pallas_call(
        functools.partial(pool_kernel, bag),
        grid=(last - first,),
        in_specs=[
            pl.BlockSpec((LANES * bag,), lambda c: (order(c + first),), memory_space=pltpu.SMEM),
            pl.BlockSpec((1, table_rows, emb), lambda c: (table, 0, 0), pipeline_mode=pl.Buffered(1)),
        ]
        + [pl.BlockSpec(memory_space=pl.ANY)] * len(more),
        out_specs=pl.BlockSpec((LANES, emb), lambda c: (c + first, 0)),
        out_shape=jax.ShapeDtypeStruct((blocks * LANES, emb), jnp.bfloat16),
        scratch_shapes=[
            pltpu.VMEM((table_rows + 8, emb), jnp.float32),
            pltpu.VMEM((LANES, emb), jnp.float32),
        ],
        input_output_aliases={2: 0} if more else {},
        compiler_params=pltpu.CompilerParams(vmem_limit_bytes=VMEM_BYTES),
        cost_estimate=pl.CostEstimate(
            flops=(last - first) * LANES * bag * emb,
            bytes_accessed=(last - first) * 100_000,
            transcendentals=0,
        ),
        name="pool",
    )(ids, tables, *more)


def items_kernel(users, ids_ref, row_ref, bank_ref, lq_ref, *refs):
    out_ref, low, high, part_low, part_high = refs
    count = ids_ref.shape[0]
    owned, width = bank_ref.shape
    items, blocks = lq_ref.shape
    unroll = 16
    step = 256

    def widen(i, carry):
        at = pl.ds(pl.multiple_of(i * step, step), step)
        both = bank_ref[at, :].astype(jnp.float32)
        low[at, :] = both[:, :LANES]
        high[at, :] = both[:, LANES:]
        return carry

    lax.fori_loop(0, owned // step, widen, 0)
    low[pl.ds(owned, 8), :] = jnp.zeros((8, LANES), jnp.float32)
    high[pl.ds(owned, 8), :] = jnp.zeros((8, LANES), jnp.float32)
    per = users // step

    def part(c, carry):
        start = c * step

        def group(g, inner):
            base = pl.multiple_of(g * unroll, unroll)
            for j in range(unroll):
                at = ids_ref[start + base + j]
                part_low[pl.ds(base + j, 1), :] = low[pl.ds(at, 1), :]
                part_high[pl.ds(base + j, 1), :] = high[pl.ds(at, 1), :]
            return inner

        lax.fori_loop(0, step // unroll, group, 0)
        at = pl.ds(pl.multiple_of((c % per) * step, 16), step)
        out_ref[c // per, at, :] = jnp.concatenate([part_low[...], part_high[...]], axis=1).astype(jnp.bfloat16)
        return carry

    lax.fori_loop(0, count // step, part, 0)
    for block in range(count // users):
        lines = []
        for c in range(per):
            ids = row_ref[:, pl.ds(block * users + c * step, step)]
            spot = lax.broadcasted_iota(jnp.int32, (blocks, step), 0)
            shift = jnp.int32(items.bit_length() - 1)
            one_hot = jnp.where(spot == lax.shift_right_arithmetic(ids, shift), 1.0, 0.0)
            by_item = jnp.dot(lq_ref[...], one_hot.astype(jnp.bfloat16), preferred_element_type=jnp.float32)
            spot = lax.broadcasted_iota(jnp.int32, (items, step), 0)
            kept = jnp.where(spot == (ids & (items - 1)), by_item, 0.0)
            lines.append(jnp.sum(kept, axis=0, keepdims=True))
        lines.append(jnp.zeros((LQ_ROWS - per, step), jnp.float32))
        out_ref[block, pl.ds(users, LQ_ROWS), :] = jnp.concatenate(lines, axis=0).astype(jnp.bfloat16)


def held_items(ids, users, bank, log_q):
    count = ids.shape[0]
    owned, width = bank.shape
    held = (ids >= 0) & (ids < owned)
    out = jax.ShapeDtypeStruct((count // users, users + LQ_ROWS, width), jnp.bfloat16)
    return pl.pallas_call(
        functools.partial(items_kernel, users),
        in_specs=[pl.BlockSpec(memory_space=pltpu.SMEM)] + [pl.BlockSpec(memory_space=pltpu.VMEM)] * 3,
        out_specs=pl.BlockSpec(memory_space=pltpu.VMEM),
        out_shape=out,
        scratch_shapes=[
            pltpu.VMEM((owned + 8, LANES), jnp.float32),
            pltpu.VMEM((owned + 8, LANES), jnp.float32),
            pltpu.VMEM((256, LANES), jnp.float32),
            pltpu.VMEM((256, LANES), jnp.float32),
        ],
        compiler_params=pltpu.CompilerParams(vmem_limit_bytes=ITEM_BYTES),
        cost_estimate=pl.CostEstimate(flops=0, bytes_accessed=30_000_000, transcendentals=0),
        name="held_items",
    )(jnp.where(held, ids, owned), ids[None, :], bank, log_q.T)


def tower_kernel(scale, lead, n_x, n_w, n_noise, apart, table_of_ref, count_ref, place_ref, *refs):
    x_refs, refs = refs[:n_x], refs[n_x:]
    owners, users, emb = x_refs[0].shape
    w_refs, refs = refs[:n_w], refs[n_w:]
    b_ref, w2_ref, *refs = refs
    pos_refs, refs = refs[:owners], refs[owners:]
    noise_refs, refs = refs[:n_noise], refs[n_noise:]
    n_grad = owners if apart else 1
    grad_refs, refs = refs[:n_grad], refs[n_grad:]
    loss_ref, w_ref, pre_ref, score_ref, noise_vec, noise_lq, picked_lq, w_sem = refs
    depth = n_x * emb
    held, width = pos_refs[0].shape
    batch_users = held - LQ_ROWS
    nnoise = noise_vec.shape[0]
    items = nnoise // picked_lq.shape[0]
    most = MOST * items

    def place(o, i, table):
        return pltpu.make_async_copy(
            w_refs[o].at[pl.ds(i * emb, emb), :],
            w_ref.at[pl.ds(pl.multiple_of(table * emb, emb), emb), :],
            w_sem.at[table],
        )

    per = w_refs[0].shape[0] // emb
    for o in range(n_w):
        for i in range(per):
            place(o, i, table_of_ref[(place_ref[1] ^ o) * per + i]).start()
    filled = jnp.int32(0)
    step = most + LQ_ROWS
    for o, (noise_ref, begin) in enumerate((r, c) for r in noise_refs for c in range(0, r.shape[0], step)):
        noise_lq[...] = noise_ref[pl.ds(begin + most, LQ_ROWS), :LANES].astype(jnp.float32)
        used = count_ref[o]

        def fill(k, carry, noise_ref=noise_ref, begin=begin, filled=filled):
            n = filled + k
            start = pl.multiple_of(begin + k * items, 16)
            noise_vec[pl.ds(pl.multiple_of(n * items, items), items), :] = noise_ref[pl.ds(start, items), :]
            picked_lq[pl.ds(n, 1), :] = noise_lq[pl.ds(k, 1), :]
            return carry

        lax.fori_loop(0, used, fill, 0)
        filled = filled + used
    def weight(s):
        return w_ref[pl.ds(pl.multiple_of(s * depth, depth), depth), :]

    pre = jnp.broadcast_to(b_ref[...], pre_ref.shape)
    for s in range(owners):
        x = jnp.concatenate([r[s] for r in x_refs], axis=1)
        for table in range(s * n_x, (s + 1) * n_x):
            place(0, 0, table).wait()
        pre = pre + jnp.dot(x, weight(s), preferred_element_type=jnp.float32)
    pre_ref[...] = pre
    hidden = (pre * jax.nn.sigmoid(pre)).astype(jnp.bfloat16)
    user_vec = jnp.dot(hidden, w2_ref[...], preferred_element_type=jnp.float32).astype(jnp.bfloat16)
    tile = 512
    spans = []
    for ref in pos_refs:
        lines = ref[pl.ds(batch_users, LQ_ROWS), :].astype(jnp.float32)
        line = jnp.concatenate([lines[i : i + 1, :] for i in range(batch_users // width)], axis=1)
        for c in range(0, batch_users, tile):
            spans.append((ref, c, line[:, c : c + tile]))
    for c in range(0, nnoise, tile):
        rows = [picked_lq[pl.ds(n, 1), :][:, :items] for n in range(c // items, (c + tile) // items)]
        spans.append((noise_vec, c, jnp.concatenate(rows, axis=1)))
    top = None
    for n, (vec, c, bias) in enumerate(spans):
        s = lax.dot_general(user_vec, vec[pl.ds(c, tile), :], CONTRACT, preferred_element_type=jnp.float32)
        s = (s * scale - bias) * LOG2E
        score_ref[:, n * tile : (n + 1) * tile] = s
        for k in range(0, tile, LANES):
            piece = s[:, k : k + LANES]
            top = piece if top is None else jnp.maximum(top, piece)
    top = jnp.max(top, axis=1, keepdims=True)
    mixed = jnp.zeros((users, width), jnp.float32)
    denom = jnp.zeros((users, LANES), jnp.float32)
    for n, (vec, c, _) in enumerate(spans):
        p = jnp.exp2(score_ref[:, n * tile : (n + 1) * tile] - top)
        for k in range(0, tile, LANES):
            denom = denom + p[:, k : k + LANES]
        mixed = mixed + jnp.dot(p.astype(jnp.bfloat16), vec[pl.ds(c, tile), :], preferred_element_type=jnp.float32)
    denom = jnp.sum(denom, axis=1, keepdims=True)
    own = pos_refs[0][pl.ds(lead, users), :].astype(jnp.float32)
    own_dot = jnp.sum(user_vec.astype(jnp.float32) * own, axis=1, keepdims=True) * scale
    loss_ref[...] = (top + jnp.log2(denom)) * LN2 - own_dot
    user_grad = ((mixed / denom - own) * scale).astype(jnp.bfloat16)
    hidden_grad = lax.dot_general(user_grad, w2_ref[...], CONTRACT, preferred_element_type=jnp.float32)
    pre = pre_ref[...]
    sig = jax.nn.sigmoid(pre)
    pre_grad = (hidden_grad * sig * (1.0 + pre * (1.0 - sig))).astype(jnp.bfloat16)
    for s in range(owners):
        part = weight(place_ref[0] ^ s if apart else s)
        grad = lax.dot_general(pre_grad, part, CONTRACT, preferred_element_type=jnp.float32).astype(jnp.bfloat16)
        if apart:
            grad_refs[s][...] = grad
        else:
            grad_refs[0][s] = grad


def tower(lead, users, apart, table_of, counts, place, xs, ws, b, w2, pos, noise, n_noise, n_picked):
    owners, _, emb = xs[0][0].shape
    per_owner = len(xs)
    hid, width = w2.shape
    depth = owners * per_owner * emb
    candidates = owners * (pos[0].shape[0] - LQ_ROWS) + n_noise
    once = pl.Buffered(1)
    smem = pl.BlockSpec(memory_space=pltpu.SMEM)
    flops = 2 * users * (2 * depth * hid + 2 * hid * width + 2 * candidates * width)
    wide = per_owner * emb
    shapes = [(users, wide)] * owners if apart else [(owners, users, wide)]
    return pl.pallas_call(
        functools.partial(tower_kernel, width ** (-0.5), lead, per_owner, len(ws), len(noise), apart),
        grid=(1,),
        in_specs=[smem] * 3
        + [
            pl.BlockSpec((owners, users, emb), lambda i, at=at: (0, at, 0), pipeline_mode=once) for _, at in xs
        ]
        + [pl.BlockSpec(memory_space=pl.ANY)] * len(ws)
        + [pl.BlockSpec(a.shape, lambda i: (0, 0), pipeline_mode=once) for a in (b, w2, *pos, *noise)],
        out_specs=[pl.BlockSpec(shape, lambda i, n=len(shape): (0,) * n) for shape in shapes]
        + [pl.BlockSpec((users, 1), lambda i: (0, 0))],
        out_shape=[jax.ShapeDtypeStruct(shape, jnp.bfloat16) for shape in shapes]
        + [jax.ShapeDtypeStruct((users, 1), jnp.float32)],
        scratch_shapes=[
            pltpu.VMEM((depth, hid), jnp.bfloat16),
            pltpu.VMEM((users, hid), jnp.float32),
            pltpu.VMEM((users, candidates), jnp.float32),
            pltpu.VMEM((n_noise, width), jnp.bfloat16),
            pltpu.VMEM((LQ_ROWS, LANES), jnp.float32),
            pltpu.VMEM((n_picked, LANES), jnp.float32),
            pltpu.SemaphoreType.DMA((depth // emb,)),
        ],
        compiler_params=pltpu.CompilerParams(vmem_limit_bytes=VMEM_BYTES),
        cost_estimate=pl.CostEstimate(
            flops=flops, bytes_accessed=60_000_000, transcendentals=users * candidates
        ),
        name="tower",
    )(table_of, counts, place, *(x for x, _ in xs), *ws, b, w2, *pos, *noise)


def swap(x, axis, offset):
    size = lax.axis_size(axis)
    return lax.ppermute(x, axis, [(i, i ^ offset) for i in range(size)])


class Spread:
    def __init__(self, x, axis):
        self.axis, self.size = axis, lax.axis_size(axis)
        self.offset = self.size // 2
        self.got, self.fresh, self.sent = {0: x}, [0], {}

    def send(self, tied=()):
        self.got.update(zip(self.sent, tied))
        sent = {}
        if self.offset > 1:
            sent = {o | self.offset: swap(v, self.axis, self.offset) for o, v in self.got.items() if not o & 1}
        sent.update({o | 1: swap(self.got[o], self.axis, 1) for o in self.fresh})
        self.fresh = [o for o in sent if not o & 1]
        self.offset //= 2
        self.sent = sent
        return list(sent.values())

    def finish(self, tied=()):
        values = self.send(tied)
        while self.sent:
            values = self.send(values)
        return [self.got[o] for o in range(self.size)]


def tie(*values):
    return lax.optimization_barrier(values)


def on_device(
    tables,
    feature_ids,
    bag_lengths,
    feature_slot,
    w_first,
    b_first,
    w_second,
    bank,
    log_q,
    noise_lists,
    pos_items,
):
    row_users, per_owner, bag = feature_ids.shape
    _, table_rows, emb = tables.shape
    owners = lax.axis_size("table")
    me = lax.axis_index("table")
    blocks_dev, block_items, width = bank.shape
    users = row_users // owners

    place = jnp.stack([me, lax.axis_index("batch")]).astype(jnp.int32)

    copies = jnp.broadcast_to(pos_items[None, :], (owners, users))
    item_ids = lax.all_to_all(copies, "table", split_axis=0, concat_axis=0, tiled=True).reshape(-1)
    sample = noise_lists[0]
    owner_of = sample // blocks_dev
    same = owner_of[:, None] == owner_of[None, :]
    index = jnp.arange(sample.shape[0], dtype=jnp.int32)
    rank = jnp.sum((same & (index[None, :] < index[:, None])).astype(jnp.int32), axis=1)
    npos = owner_of * MOST + rank
    pick = (npos[None, :] == (me * MOST + jnp.arange(MOST, dtype=jnp.int32))[:, None]).astype(jnp.int32)
    local_block = jnp.sum(pick * (sample - me * blocks_dev)[None, :], axis=1)
    noise_lq = jnp.pad(log_q[local_block], ((0, LQ_ROWS - MOST), (0, width - block_items)))
    my_noise = jnp.concatenate([bank[local_block].reshape(MOST * block_items, width), noise_lq], axis=0)
    item_ids, my_noise, w_part = tie(item_ids, my_noise, w_first)
    w_rounds = Spread(w_part, "batch")
    w_got = w_rounds.send()
    near_noise, noise_from, offset = [my_noise], [0], owners // 2
    noise_got = [swap(my_noise, "table", offset)]
    owned = blocks_dev * block_items
    mine = held_items(item_ids - me * owned, users, bank.reshape(owned, width), log_q)

    by_table = jnp.transpose(feature_ids, (1, 2, 0))
    used = jnp.arange(bag, dtype=jnp.int32)[None, :, None] < jnp.transpose(bag_lengths, (1, 0))[:, None, :]
    by_table = jnp.where(used, by_table, table_rows)
    by_table = by_table.reshape(per_owner, bag, row_users // LANES, LANES)
    by_table = jnp.transpose(by_table, (0, 2, 1, 3)).reshape(per_owner, row_users * bag)
    ids = [by_table[j] for j in range(per_owner)]
    blocks = row_users // LANES
    block_users = users // LANES
    part_blocks = block_users // 2
    half = blocks // 2

    def straight(c):
        return c

    def halves(c):
        h, c = c // half, c % half
        return c // part_blocks * block_users + h * part_blocks + c % part_blocks

    def exchange(pooled):
        pooled = pooled.reshape(owners, -1, emb)
        return lax.all_to_all(pooled, "table", split_axis=0, concat_axis=0, tiled=True)

    mine, tables, noise_got, *ids = tie(mine, tables, noise_got, *ids)

    def more_noise():
        near_noise.extend(noise_got)
        noise_from.extend([o ^ offset for o in noise_from])

    mine = lax.all_to_all(mine, "table", split_axis=0, concat_axis=0, tiled=True)
    while offset > 2:
        more_noise()
        offset //= 2
        noise_got = [swap(v, "table", offset) for v in near_noise]
    first_noise = swap(jnp.concatenate(near_noise, axis=0), "table", 1)
    pooled = pool(ids[0], tables, 0, bag, straight, 0, blocks, blocks, None)
    whole = [pooled]
    for j in range(1, per_owner - 1):
        tables, pooled = tie(tables, pooled)
        pooled = pool(ids[j], tables, j, bag, straight, 0, blocks, blocks, None)
        whole.append(pooled)

    tables, whole, mine, noise_got, first_noise, w_got = tie(tables, whole, mine, noise_got, first_noise, w_got)
    w_got = w_rounds.send(w_got)
    more_noise()
    far_noise = swap(jnp.concatenate(noise_got, axis=0), "table", 1)
    near_noise = jnp.concatenate(near_noise, axis=0)
    own_pos = jnp.sum(mine.astype(jnp.float32), axis=0).astype(jnp.bfloat16)
    own_pos, tables = tie(own_pos, tables)
    pos_rounds = Spread(own_pos, "table")
    got = pos_rounds.send()

    last = ids[-1]
    final = functools.partial(pool, tables=tables, table=per_owner - 1, bag=bag, order=halves, blocks=blocks)
    cut = blocks // 4
    pooled = final(ids=last, first=0, last=cut, given=None)
    pooled, whole, got, far_noise, last = tie(pooled, whole, got, far_noise, last)
    xs = [exchange(v) for v in whole]
    got = pos_rounds.send(got)
    pooled = final(ids=last, first=cut, last=blocks - cut, given=pooled)
    pooled, xs, got, last = tie(pooled, xs, got, last)
    early = exchange(pooled[: row_users // 2])
    got = pos_rounds.send(got)
    pooled = final(ids=last, first=blocks - cut, last=blocks, given=pooled)
    pooled, early, got = tie(pooled, early, got)
    late = exchange(pooled[row_users // 2 :])
    pos = pos_rounds.finish(got)
    ws = w_rounds.finish(w_got)

    slots = jnp.arange(feature_slot.shape[0], dtype=jnp.int32)
    table_of = jnp.sum(jnp.where(feature_slot[None, :] == slots[:, None], slots[None, :], 0), axis=1)
    noise_owner = me ^ jnp.asarray(noise_from + [o ^ 1 for o in noise_from], jnp.int32)
    counts = jnp.sum((owner_of[None, :] == noise_owner[:, None]).astype(jnp.int32), axis=1)
    run = functools.partial(
        tower, users=users // 2, table_of=table_of, counts=counts, place=place, ws=ws, b=b_first[None, :], w2=w_second, pos=pos,
        noise=[near_noise, first_noise, far_noise], n_noise=sample.shape[0] * block_items, n_picked=sample.shape[0],
    )
    grad_early, loss_early = run(lead=0, apart=False, xs=[(v, 0) for v in xs] + [(early, 0)])
    back = [lax.all_to_all(grad_early, "table", split_axis=0, concat_axis=0, tiled=True)]
    _, late = tie(loss_early, late)
    *grad_late, loss_late = run(lead=users // 2, apart=True, xs=[(v, 1) for v in xs] + [(late, 0)])
    came = {o: grad_late[o] if o == 0 else swap(grad_late[o], "table", o) for o in reversed(range(owners))}
    both = jnp.concatenate([back[0], jnp.zeros_like(back[0])], axis=1)
    for o in range(owners):
        both = lax.dynamic_update_slice(both, came[o][None], (me ^ o, users // 2, 0))
    losses = [loss_early[:, 0], loss_late[:, 0]]
    own_lq = own_pos[users : users + users // width].astype(jnp.float32).reshape(users)
    grad = both.reshape(row_users, per_owner, emb)
    return (jnp.concatenate(losses) + own_lq, grad)


def solution(mesh):
    return jax.shard_map(
        on_device,
        mesh=mesh,
        in_specs=(
            P("table", None, None),
            P("batch", "table", None),
            P("batch", "table"),
            P(),
            P("batch", None),
            P(),
            P(),
            P("table", None, None),
            P("table", None),
            P("batch", None),
            P(("batch", "table")),
        ),
        out_specs=(P(("batch", "table")), P("batch", "table", None)),
        check_vma=False,
    )
```

```python
import functools
import math

import jax
import jax.numpy as jnp
from jax import lax
from jax.experimental import pallas as pl
from jax.experimental.pallas import tpu as pltpu
from jax.sharding import PartitionSpec as P

MOST = 8
LANES = 128
LQ_ROWS = 16
VMEM_BYTES = 52 << 20
ITEM_BYTES = 24 << 20
CONTRACT = (((1,), (1,)), ((), ()))
LOG2E = math.log2(math.e)
LN2 = math.log(2.0)


def whole(shape):
    return pl.BlockSpec(shape, lambda *_: (0,) * len(shape))


def pool_kernel(bag, ids_ref, table_ref, *refs):
    out_ref, wide, rows = refs[-3:]
    table_rows = table_ref.shape[1]
    unroll = 32

    @pl.when(pl.program_id(0) == 0)
    def _():
        def widen(i, carry):
            at = pl.ds(pl.multiple_of(i * 256, 256), 256)
            wide[at, :] = table_ref[0, at, :].astype(jnp.float32)
            return carry

        lax.fori_loop(0, table_rows // 256, widen, 0)
        wide[pl.ds(table_rows, 8), :] = jnp.zeros((8, LANES), jnp.float32)

    def group(g, carry):
        base = pl.multiple_of(g * unroll, unroll)
        for j in range(unroll):
            got = [wide[pl.ds(ids_ref[base + (k * LANES + j)], 1), :] for k in range(bag)]
            while len(got) > 1:
                got = [got[i] + got[i + 1] for i in range(0, len(got), 2)]
            rows[pl.ds(base + j, 1), :] = got[0]
        return carry

    lax.fori_loop(0, LANES // unroll, group, 0)
    out_ref[...] = rows[...].astype(jnp.bfloat16)


def pool(ids, tables, table, bag, order, first, last, blocks, given):
    _, table_rows, emb = tables.shape
    more = [] if given is None else [given]
    return pl.pallas_call(
        functools.partial(pool_kernel, bag),
        grid=(last - first,),
        in_specs=[
            pl.BlockSpec((LANES * bag,), lambda c: (order(c + first),), memory_space=pltpu.SMEM),
            pl.BlockSpec((1, table_rows, emb), lambda c: (table, 0, 0), pipeline_mode=pl.Buffered(1)),
        ]
        + [pl.BlockSpec(memory_space=pl.ANY)] * len(more),
        out_specs=pl.BlockSpec((LANES, emb), lambda c: (c + first, 0)),
        out_shape=jax.ShapeDtypeStruct((blocks * LANES, emb), jnp.bfloat16),
        scratch_shapes=[
            pltpu.VMEM((table_rows + 8, emb), jnp.float32),
            pltpu.VMEM((LANES, emb), jnp.float32),
        ],
        input_output_aliases={2: 0} if more else {},
        compiler_params=pltpu.CompilerParams(vmem_limit_bytes=VMEM_BYTES),
        cost_estimate=pl.CostEstimate(
            flops=(last - first) * LANES * bag * emb,
            bytes_accessed=(last - first) * 100_000,
            transcendentals=0,
        ),
        name="pool",
    )(ids, tables, *more)


def items_kernel(users, ids_ref, row_ref, bank_ref, lq_ref, *refs):
    out_ref, low, high, part_low, part_high = refs
    count = ids_ref.shape[0]
    owned, width = bank_ref.shape
    items, blocks = lq_ref.shape
    unroll = 16
    step = 256

    def widen(i, carry):
        at = pl.ds(pl.multiple_of(i * step, step), step)
        both = bank_ref[at, :].astype(jnp.float32)
        low[at, :] = both[:, :LANES]
        high[at, :] = both[:, LANES:]
        return carry

    lax.fori_loop(0, owned // step, widen, 0)
    low[pl.ds(owned, 8), :] = jnp.zeros((8, LANES), jnp.float32)
    high[pl.ds(owned, 8), :] = jnp.zeros((8, LANES), jnp.float32)
    per = users // step

    def part(c, carry):
        start = c * step

        def group(g, inner):
            base = pl.multiple_of(g * unroll, unroll)
            for j in range(unroll):
                at = ids_ref[start + base + j]
                part_low[pl.ds(base + j, 1), :] = low[pl.ds(at, 1), :]
                part_high[pl.ds(base + j, 1), :] = high[pl.ds(at, 1), :]
            return inner

        lax.fori_loop(0, step // unroll, group, 0)
        at = pl.ds(pl.multiple_of((c % per) * step, 16), step)
        out_ref[c // per, at, :] = jnp.concatenate([part_low[...], part_high[...]], axis=1).astype(jnp.bfloat16)
        return carry

    lax.fori_loop(0, count // step, part, 0)
    for block in range(count // users):
        lines = []
        for c in range(per):
            ids = row_ref[:, pl.ds(block * users + c * step, step)]
            spot = lax.broadcasted_iota(jnp.int32, (blocks, step), 0)
            shift = jnp.int32(items.bit_length() - 1)
            one_hot = jnp.where(spot == lax.shift_right_arithmetic(ids, shift), 1.0, 0.0)
            by_item = jnp.dot(lq_ref[...], one_hot.astype(jnp.bfloat16), preferred_element_type=jnp.float32)
            spot = lax.broadcasted_iota(jnp.int32, (items, step), 0)
            kept = jnp.where(spot == (ids & (items - 1)), by_item, 0.0)
            lines.append(jnp.sum(kept, axis=0, keepdims=True))
        lines.append(jnp.zeros((LQ_ROWS - per, step), jnp.float32))
        out_ref[block, pl.ds(users, LQ_ROWS), :] = jnp.concatenate(lines, axis=0).astype(jnp.bfloat16)


def held_items(ids, users, bank, log_q):
    count = ids.shape[0]
    owned, width = bank.shape
    held = (ids >= 0) & (ids < owned)
    out = jax.ShapeDtypeStruct((count // users, users + LQ_ROWS, width), jnp.bfloat16)
    return pl.pallas_call(
        functools.partial(items_kernel, users),
        in_specs=[pl.BlockSpec(memory_space=pltpu.SMEM)] + [pl.BlockSpec(memory_space=pltpu.VMEM)] * 3,
        out_specs=pl.BlockSpec(memory_space=pltpu.VMEM),
        out_shape=out,
        scratch_shapes=[
            pltpu.VMEM((owned + 8, LANES), jnp.float32),
            pltpu.VMEM((owned + 8, LANES), jnp.float32),
            pltpu.VMEM((256, LANES), jnp.float32),
            pltpu.VMEM((256, LANES), jnp.float32),
        ],
        compiler_params=pltpu.CompilerParams(vmem_limit_bytes=ITEM_BYTES),
        cost_estimate=pl.CostEstimate(flops=0, bytes_accessed=30_000_000, transcendentals=0),
        name="held_items",
    )(jnp.where(held, ids, owned), ids[None, :], bank, log_q.T)


def tower_kernel(scale, lead, n_x, n_w, n_noise, apart, table_of_ref, count_ref, place_ref, *refs):
    x_refs, refs = refs[:n_x], refs[n_x:]
    owners, users, emb = x_refs[0].shape
    w_refs, refs = refs[:n_w], refs[n_w:]
    b_ref, w2_ref, *refs = refs
    pos_refs, refs = refs[:owners], refs[owners:]
    noise_refs, refs = refs[:n_noise], refs[n_noise:]
    n_grad = owners if apart else 1
    grad_refs, refs = refs[:n_grad], refs[n_grad:]
    loss_ref, w_ref, pre_ref, score_ref, noise_vec, noise_lq, picked_lq, w_sem = refs
    depth = n_x * emb
    held, width = pos_refs[0].shape
    batch_users = held - LQ_ROWS
    nnoise = noise_vec.shape[0]
    items = nnoise // picked_lq.shape[0]
    most = MOST * items

    def place(o, i, table):
        return pltpu.make_async_copy(
            w_refs[o].at[pl.ds(i * emb, emb), :],
            w_ref.at[pl.ds(pl.multiple_of(table * emb, emb), emb), :],
            w_sem.at[table],
        )

    per = w_refs[0].shape[0] // emb
    for o in range(n_w):
        for i in range(per):
            place(o, i, table_of_ref[(place_ref[1] ^ o) * per + i]).start()
    filled = jnp.int32(0)
    step = most + LQ_ROWS
    for o, (noise_ref, begin) in enumerate((r, c) for r in noise_refs for c in range(0, r.shape[0], step)):
        noise_lq[...] = noise_ref[pl.ds(begin + most, LQ_ROWS), :LANES].astype(jnp.float32)
        used = count_ref[o]

        def fill(k, carry, noise_ref=noise_ref, begin=begin, filled=filled):
            n = filled + k
            start = pl.multiple_of(begin + k * items, 16)
            noise_vec[pl.ds(pl.multiple_of(n * items, items), items), :] = noise_ref[pl.ds(start, items), :]
            picked_lq[pl.ds(n, 1), :] = noise_lq[pl.ds(k, 1), :]
            return carry

        lax.fori_loop(0, used, fill, 0)
        filled = filled + used
    def weight(s):
        return w_ref[pl.ds(pl.multiple_of(s * depth, depth), depth), :]

    pre = jnp.broadcast_to(b_ref[...], pre_ref.shape)
    for s in range(owners):
        x = jnp.concatenate([r[s] for r in x_refs], axis=1)
        for table in range(s * n_x, (s + 1) * n_x):
            place(0, 0, table).wait()
        pre = pre + jnp.dot(x, weight(s), preferred_element_type=jnp.float32)
    pre_ref[...] = pre
    hidden = (pre * jax.nn.sigmoid(pre)).astype(jnp.bfloat16)
    user_vec = jnp.dot(hidden, w2_ref[...], preferred_element_type=jnp.float32).astype(jnp.bfloat16)
    tile = 512
    spans = []
    for ref in pos_refs:
        lines = ref[pl.ds(batch_users, LQ_ROWS), :].astype(jnp.float32)
        line = jnp.concatenate([lines[i : i + 1, :] for i in range(batch_users // width)], axis=1)
        for c in range(0, batch_users, tile):
            spans.append((ref, c, line[:, c : c + tile]))
    for c in range(0, nnoise, tile):
        rows = [picked_lq[pl.ds(n, 1), :][:, :items] for n in range(c // items, (c + tile) // items)]
        spans.append((noise_vec, c, jnp.concatenate(rows, axis=1)))
    top = None
    for n, (vec, c, bias) in enumerate(spans):
        s = lax.dot_general(user_vec, vec[pl.ds(c, tile), :], CONTRACT, preferred_element_type=jnp.float32)
        s = (s * scale - bias) * LOG2E
        score_ref[:, n * tile : (n + 1) * tile] = s
        for k in range(0, tile, LANES):
            piece = s[:, k : k + LANES]
            top = piece if top is None else jnp.maximum(top, piece)
    top = jnp.max(top, axis=1, keepdims=True)
    mixed = jnp.zeros((users, width), jnp.float32)
    denom = jnp.zeros((users, LANES), jnp.float32)
    for n, (vec, c, _) in enumerate(spans):
        p = jnp.exp2(score_ref[:, n * tile : (n + 1) * tile] - top)
        for k in range(0, tile, LANES):
            denom = denom + p[:, k : k + LANES]
        mixed = mixed + jnp.dot(p.astype(jnp.bfloat16), vec[pl.ds(c, tile), :], preferred_element_type=jnp.float32)
    denom = jnp.sum(denom, axis=1, keepdims=True)
    own = pos_refs[0][pl.ds(lead, users), :].astype(jnp.float32)
    own_dot = jnp.sum(user_vec.astype(jnp.float32) * own, axis=1, keepdims=True) * scale
    loss_ref[...] = (top + jnp.log2(denom)) * LN2 - own_dot
    user_grad = ((mixed / denom - own) * scale).astype(jnp.bfloat16)
    hidden_grad = lax.dot_general(user_grad, w2_ref[...], CONTRACT, preferred_element_type=jnp.float32)
    pre = pre_ref[...]
    sig = jax.nn.sigmoid(pre)
    pre_grad = (hidden_grad * sig * (1.0 + pre * (1.0 - sig))).astype(jnp.bfloat16)
    for s in range(owners):
        part = weight(place_ref[0] ^ s if apart else s)
        grad = lax.dot_general(pre_grad, part, CONTRACT, preferred_element_type=jnp.float32).astype(jnp.bfloat16)
        if apart:
            grad_refs[s][...] = grad
        else:
            grad_refs[0][s] = grad


def tower(lead, users, apart, table_of, counts, place, xs, ws, b, w2, pos, noise, n_noise, n_picked):
    owners, _, emb = xs[0][0].shape
    per_owner = len(xs)
    hid, width = w2.shape
    depth = owners * per_owner * emb
    candidates = owners * (pos[0].shape[0] - LQ_ROWS) + n_noise
    once = pl.Buffered(1)
    smem = pl.BlockSpec(memory_space=pltpu.SMEM)
    flops = 2 * users * (2 * depth * hid + 2 * hid * width + 2 * candidates * width)
    wide = per_owner * emb
    shapes = [(users, wide)] * owners if apart else [(owners, users, wide)]
    return pl.pallas_call(
        functools.partial(tower_kernel, width ** (-0.5), lead, per_owner, len(ws), len(noise), apart),
        grid=(1,),
        in_specs=[smem] * 3
        + [
            pl.BlockSpec((owners, users, emb), lambda i, at=at: (0, at, 0), pipeline_mode=once) for _, at in xs
        ]
        + [pl.BlockSpec(memory_space=pl.ANY)] * len(ws)
        + [pl.BlockSpec(a.shape, lambda i: (0, 0), pipeline_mode=once) for a in (b, w2, *pos, *noise)],
        out_specs=[pl.BlockSpec(shape, lambda i, n=len(shape): (0,) * n) for shape in shapes]
        + [pl.BlockSpec((users, 1), lambda i: (0, 0))],
        out_shape=[jax.ShapeDtypeStruct(shape, jnp.bfloat16) for shape in shapes]
        + [jax.ShapeDtypeStruct((users, 1), jnp.float32)],
        scratch_shapes=[
            pltpu.VMEM((depth, hid), jnp.bfloat16),
            pltpu.VMEM((users, hid), jnp.float32),
            pltpu.VMEM((users, candidates), jnp.float32),
            pltpu.VMEM((n_noise, width), jnp.bfloat16),
            pltpu.VMEM((LQ_ROWS, LANES), jnp.float32),
            pltpu.VMEM((n_picked, LANES), jnp.float32),
            pltpu.SemaphoreType.DMA((depth // emb,)),
        ],
        compiler_params=pltpu.CompilerParams(vmem_limit_bytes=VMEM_BYTES),
        cost_estimate=pl.CostEstimate(
            flops=flops, bytes_accessed=60_000_000, transcendentals=users * candidates
        ),
        name="tower",
    )(table_of, counts, place, *(x for x, _ in xs), *ws, b, w2, *pos, *noise)


def swap(x, axis, offset):
    size = lax.axis_size(axis)
    return lax.ppermute(x, axis, [(i, i ^ offset) for i in range(size)])


class Spread:
    def __init__(self, x, axis):
        self.axis, self.size = axis, lax.axis_size(axis)
        self.offset = self.size // 2
        self.got, self.fresh, self.sent = {0: x}, [0], {}

    def send(self, tied=()):
        self.got.update(zip(self.sent, tied))
        sent = {}
        if self.offset > 1:
            sent = {o | self.offset: swap(v, self.axis, self.offset) for o, v in self.got.items() if not o & 1}
        sent.update({o | 1: swap(self.got[o], self.axis, 1) for o in self.fresh})
        self.fresh = [o for o in sent if not o & 1]
        self.offset //= 2
        self.sent = sent
        return list(sent.values())

    def finish(self, tied=()):
        values = self.send(tied)
        while self.sent:
            values = self.send(values)
        return [self.got[o] for o in range(self.size)]


def tie(*values):
    return lax.optimization_barrier(values)


def on_device(
    tables,
    feature_ids,
    bag_lengths,
    feature_slot,
    w_first,
    b_first,
    w_second,
    bank,
    log_q,
    noise_lists,
    pos_items,
):
    row_users, per_owner, bag = feature_ids.shape
    _, table_rows, emb = tables.shape
    owners = lax.axis_size("table")
    me = lax.axis_index("table")
    blocks_dev, block_items, width = bank.shape
    users = row_users // owners

    place = jnp.stack([me, lax.axis_index("batch")]).astype(jnp.int32)

    copies = jnp.broadcast_to(pos_items[None, :], (owners, users))
    item_ids = lax.all_to_all(copies, "table", split_axis=0, concat_axis=0, tiled=True).reshape(-1)
    sample = noise_lists[0]
    owner_of = sample // blocks_dev
    same = owner_of[:, None] == owner_of[None, :]
    index = jnp.arange(sample.shape[0], dtype=jnp.int32)
    rank = jnp.sum((same & (index[None, :] < index[:, None])).astype(jnp.int32), axis=1)
    npos = owner_of * MOST + rank
    pick = (npos[None, :] == (me * MOST + jnp.arange(MOST, dtype=jnp.int32))[:, None]).astype(jnp.int32)
    local_block = jnp.sum(pick * (sample - me * blocks_dev)[None, :], axis=1)
    noise_lq = jnp.pad(log_q[local_block], ((0, LQ_ROWS - MOST), (0, width - block_items)))
    my_noise = jnp.concatenate([bank[local_block].reshape(MOST * block_items, width), noise_lq], axis=0)
    item_ids, my_noise, w_part = tie(item_ids, my_noise, w_first)
    w_rounds = Spread(w_part, "batch")
    w_got = w_rounds.send()
    near_noise, noise_from, offset = [my_noise], [0], owners // 2
    noise_got = [swap(my_noise, "table", offset)]
    owned = blocks_dev * block_items
    mine = held_items(item_ids - me * owned, users, bank.reshape(owned, width), log_q)

    by_table = jnp.transpose(feature_ids, (1, 2, 0))
    used = jnp.arange(bag, dtype=jnp.int32)[None, :, None] < jnp.transpose(bag_lengths, (1, 0))[:, None, :]
    by_table = jnp.where(used, by_table, table_rows)
    by_table = by_table.reshape(per_owner, bag, row_users // LANES, LANES)
    by_table = jnp.transpose(by_table, (0, 2, 1, 3)).reshape(per_owner, row_users * bag)
    ids = [by_table[j] for j in range(per_owner)]
    blocks = row_users // LANES
    block_users = users // LANES
    part_blocks = block_users // 2
    half = blocks // 2

    def straight(c):
        return c

    def halves(c):
        h, c = c // half, c % half
        return c // part_blocks * block_users + h * part_blocks + c % part_blocks

    def exchange(pooled):
        pooled = pooled.reshape(owners, -1, emb)
        return lax.all_to_all(pooled, "table", split_axis=0, concat_axis=0, tiled=True)

    mine, tables, noise_got, *ids = tie(mine, tables, noise_got, *ids)

    def more_noise():
        near_noise.extend(noise_got)
        noise_from.extend([o ^ offset for o in noise_from])

    mine = lax.all_to_all(mine, "table", split_axis=0, concat_axis=0, tiled=True)
    while offset > 2:
        more_noise()
        offset //= 2
        noise_got = [swap(v, "table", offset) for v in near_noise]
    first_noise = swap(jnp.concatenate(near_noise, axis=0), "table", 1)
    pooled = pool(ids[0], tables, 0, bag, straight, 0, blocks, blocks, None)
    whole = [pooled]
    for j in range(1, per_owner - 1):
        tables, pooled = tie(tables, pooled)
        pooled = pool(ids[j], tables, j, bag, straight, 0, blocks, blocks, None)
        whole.append(pooled)

    tables, whole, mine, noise_got, first_noise, w_got = tie(tables, whole, mine, noise_got, first_noise, w_got)
    w_got = w_rounds.send(w_got)
    more_noise()
    far_noise = swap(jnp.concatenate(noise_got, axis=0), "table", 1)
    near_noise = jnp.concatenate(near_noise, axis=0)
    own_pos = jnp.sum(mine.astype(jnp.float32), axis=0).astype(jnp.bfloat16)
    own_pos, tables = tie(own_pos, tables)
    pos_rounds = Spread(own_pos, "table")
    got = pos_rounds.send()

    last = ids[-1]
    final = functools.partial(pool, tables=tables, table=per_owner - 1, bag=bag, order=halves, blocks=blocks)
    cut = blocks // 4
    pooled = final(ids=last, first=0, last=cut, given=None)
    pooled, whole, got, far_noise, last = tie(pooled, whole, got, far_noise, last)
    xs = [exchange(v) for v in whole]
    got = pos_rounds.send(got)
    pooled = final(ids=last, first=cut, last=blocks - cut, given=pooled)
    pooled, xs, got, last = tie(pooled, xs, got, last)
    early = exchange(pooled[: row_users // 2])
    got = pos_rounds.send(got)
    pooled = final(ids=last, first=blocks - cut, last=blocks, given=pooled)
    pooled, early, got = tie(pooled, early, got)
    late = exchange(pooled[row_users // 2 :])
    pos = pos_rounds.finish(got)
    ws = w_rounds.finish(w_got)

    slots = jnp.arange(feature_slot.shape[0], dtype=jnp.int32)
    table_of = jnp.sum(jnp.where(feature_slot[None, :] == slots[:, None], slots[None, :], 0), axis=1)
    noise_owner = me ^ jnp.asarray(noise_from + [o ^ 1 for o in noise_from], jnp.int32)
    counts = jnp.sum((owner_of[None, :] == noise_owner[:, None]).astype(jnp.int32), axis=1)
    run = functools.partial(
        tower, users=users // 2, table_of=table_of, counts=counts, place=place, ws=ws, b=b_first[None, :], w2=w_second, pos=pos,
        noise=[near_noise, first_noise, far_noise], n_noise=sample.shape[0] * block_items, n_picked=sample.shape[0],
    )
    grad_early, loss_early = run(lead=0, apart=False, xs=[(v, 0) for v in xs] + [(early, 0)])
    back = [lax.all_to_all(grad_early, "table", split_axis=0, concat_axis=0, tiled=True)]
    _, late = tie(loss_early, late)
    *grad_late, loss_late = run(lead=users // 2, apart=True, xs=[(v, 1) for v in xs] + [(late, 0)])
    first = back[0].reshape(owners, users // 2, per_owner, emb)
    both = jnp.concatenate([first, jnp.zeros_like(first)], axis=1)
    far = range(owners // 2, owners)
    came = {o: swap(grad_late[o], "table", o) for o in reversed(far)}
    both, grad_late = tie(both, grad_late[: owners // 2])
    came.update({o: grad_late[o] if o == 0 else swap(grad_late[o], "table", o) for o in range(owners // 2)})
    for o in [*far, *range(owners // 2)]:
        late_rows = came[o].reshape(1, users // 2, per_owner, emb)
        both = lax.dynamic_update_slice(both, late_rows, (me ^ o, users // 2, 0, 0))
    losses = [loss_early[:, 0], loss_late[:, 0]]
    own_lq = own_pos[users : users + users // width].astype(jnp.float32).reshape(users)
    grad = both.reshape(row_users, per_owner, emb)
    return (jnp.concatenate(losses) + own_lq, grad)


def solution(mesh):
    return jax.shard_map(
        on_device,
        mesh=mesh,
        in_specs=(
            P("table", None, None),
            P("batch", "table", None),
            P("batch", "table"),
            P(),
            P("batch", None),
            P(),
            P(),
            P("table", None, None),
            P("table", None),
            P("batch", None),
            P(("batch", "table")),
        ),
        out_specs=(P(("batch", "table")), P("batch", "table", None)),
        check_vma=False,
    )
```
